128 devices in a mesh: rep: 64 (over y, x, z_lo, core), fsdp: 2 (over z_hi).
Axes of the slice: x: 4, y: 4, z: 4 (z_hi: 2, z_lo: 2; z = z_hi * 2 + z_lo), core: 2. Of those that a mesh axis runs over, the one named last changes fastest.
Arguments:
- tokens: bfloat16 [65536, 768], P(('rep', 'fsdp')), may hold values from -6 to 6
- norm_gain_one: bfloat16 [768], P('fsdp'), may hold values from 0.099609375 to 1.8984375
- qkv_weight: bfloat16 [768, 2304], P('fsdp'), may hold values from -0.21875 to 0.21875
- attn_out_weight: bfloat16 [768, 768], P('fsdp'), may hold values from -2.5 to 2.5
- norm_gain_two: bfloat16 [768], P('fsdp'), may hold values from 0.099609375 to 1.8984375
- in_weight: bfloat16 [768, 2304], P('fsdp'), may hold values from -0.21875 to 0.21875
- mlp_out_weight: bfloat16 [1152, 768], P('fsdp'), may hold values from -0.25 to 0.25
- cotangent: bfloat16 [65536, 768], P(('rep', 'fsdp')), may hold values from -6 to 6
Outputs:
- layer_output: bfloat16 [65536, 768], P(('rep', 'fsdp'))
- token_grad: bfloat16 [65536, 768], P(('rep', 'fsdp'))
- gain_one_grad: float32 [768], P('fsdp')
- qkv_grad: float32 [768, 2304], P('fsdp')
- attn_out_grad: float32 [768, 768], P('fsdp')
- gain_two_grad: float32 [768], P('fsdp')
- in_grad: float32 [768, 2304], P('fsdp')
- mlp_out_grad: float32 [1152, 768], P('fsdp')
The draws below stay inside these ranges and needn't reach their ends.
All inputs are finite; a program needn't handle non-finite values.
Results may differ from the reference program's by a relative error of at most 0.018.
Values may be sent and summed in bfloat16 or wider, within the bound.
No kernel may reach another device: no remote copies, remote signals or barrier semaphores. Data moves between devices by JAX's collectives and lax.ppermute only.
A program may use at most 128 MiB of HBM per device.

```python
import jax
import jax.numpy as jnp
from jax import lax

D = 768
HEADS = 12
HEAD_DIM = 64
FF = 1152
HALF_WIN = 64
SEQ_LEN = 1024
SEQS = 64
TOKENS = 65536


def block_scale(rng, dims, pieces, low, largest):
    level = 1.0
    for dim, parts in pieces:
        draws = jax.random.uniform(jax.random.fold_in(jax.random.fold_in(rng, 6), dim), (parts,), jnp.float32, low / len(pieces), largest / len(pieces))
        level = level * jnp.repeat(jnp.exp(draws), dims[dim] // parts).reshape((-1,) + (1,) * (len(dims) - 1 - dim))
    return level


def normal_values(rng, shape, deviation, limit, cuts=(), kind=jnp.bfloat16):
    array = deviation * jax.random.normal(rng, shape, jnp.float32)
    if cuts:
        array = array * block_scale(rng, shape, cuts, -0.22, 0.18)
    return jnp.clip(array, -limit, limit).astype(kind)


def setup_inputs(seed: int = 0) -> dict:
    arg_keys = jax.random.split(jax.random.key(seed), 9)
    tokens = normal_values(arg_keys[0], (TOKENS, D), 1.0, 6.0, ((0, 128),))
    norm_gain_one = jnp.clip(1.0 + 0.18 * jax.random.normal(arg_keys[1], (D,), jnp.float32), 0.099609375, 1.8984375).astype(jnp.bfloat16)
    qkv_weight = normal_values(arg_keys[2], (D, 3 * D), D ** -0.5, 0.21875, ((0, 2),))
    attn_out_weight = normal_values(arg_keys[3], (D, D), (D // (2 * HALF_WIN)) ** -0.5, 2.5, ((0, 2),))
    norm_gain_two = jnp.clip(1.0 + 0.18 * jax.random.normal(arg_keys[4], (D,), jnp.float32), 0.099609375, 1.8984375).astype(jnp.bfloat16)
    in_weight = normal_values(arg_keys[5], (D, 2 * FF), D ** -0.5, 0.21875, ((0, 2),))
    mlp_out_weight = normal_values(arg_keys[6], (FF, D), (FF // 2) ** -0.5, 0.25, ((0, 2),))
    cotangent = normal_values(arg_keys[7], (TOKENS, D), 1.0, 6.0, ((0, 128),))
    return dict(tokens=tokens, norm_gain_one=norm_gain_one, qkv_weight=qkv_weight, attn_out_weight=attn_out_weight, norm_gain_two=norm_gain_two, in_weight=in_weight, mlp_out_weight=mlp_out_weight, cotangent=cotangent)


@jax.custom_vjp
def low(v):
    return lax.optimization_barrier(v.astype(jnp.bfloat16)).astype(jnp.float32)

@jax.custom_vjp
def low_back(v):
    return v

def low_keep(v):
    return (low(v), None)

def low_pass(kept, grad):
    return (grad,)

def back_keep(v):
    return (v, None)

def back_low(kept, grad):
    return (low(grad),)
low.defvjp(low_keep, low_pass)
low_back.defvjp(back_keep, back_low)
eps_norm = 1e-05
theta = 10000.0
masked_value = -1e+30

def layer_norm(values, gain):
    row_mean = lax.optimization_barrier(jnp.mean(values, axis=-1, keepdims=True))
    centred = values - row_mean
    variance = lax.optimization_barrier(jnp.mean(centred * centred, axis=-1, keepdims=True))
    return centred * lax.rsqrt(variance + eps_norm) * gain

def rotary(values, positions):
    half_dim = values.shape[-1] // 2
    frequency = theta ** (-(jnp.arange(half_dim, dtype=jnp.float32) * 2.0 / values.shape[-1]))
    angles = positions.astype(jnp.float32)[:, None] * frequency[None, :]
    cosine = jnp.concatenate([jnp.cos(angles), jnp.cos(angles)], -1)[:, None, :]
    sine = jnp.concatenate([jnp.sin(angles), jnp.sin(angles)], -1)[:, None, :]
    first_half = values[..., :half_dim]
    second = values[..., half_dim:]
    turned = jnp.concatenate([-second, first_half], -1)
    return values * cosine + turned * sine

def gelu_exact(values):
    return 0.5 * values * (1.0 + lax.erf(values * 0.7071067811865476))

def attend(queries, keys_rot, values_in):
    length = queries.shape[0]
    block_rows = min(512, length)
    block_count = length // block_rows
    score_scale = HEAD_DIM ** (-0.5)
    edges = ((HALF_WIN, HALF_WIN), (0, 0), (0, 0))
    keys_pad = jnp.pad(keys_rot, edges)
    values_pad = jnp.pad(values_in, edges)
    span = block_rows + 2 * HALF_WIN

    def one_block(block_index):
        row_start = block_index * block_rows
        query_block = lax.dynamic_slice_in_dim(queries, row_start, block_rows, 0)
        key_block = lax.dynamic_slice_in_dim(keys_pad, row_start, span, 0)
        value_block = lax.dynamic_slice_in_dim(values_pad, row_start, span, 0)
        query_pos = row_start + jnp.arange(block_rows, dtype=jnp.int32)
        key_pos = row_start - HALF_WIN + jnp.arange(span, dtype=jnp.int32)
        allowed = (jnp.abs(query_pos[:, None] - key_pos[None, :]) <= HALF_WIN) & (key_pos[None, :] >= 0) & (key_pos[None, :] < length)
        scores = jnp.einsum('qhd,khd->hqk', query_block, key_block, precision=lax.Precision.HIGHEST) * score_scale
        scores = low_back(jnp.where(allowed[None], scores, masked_value))
        top_score = lax.optimization_barrier(jnp.max(scores, axis=-1, keepdims=True))
        raised = jnp.exp(scores - top_score)
        attn_probs = raised / lax.optimization_barrier(jnp.sum(raised, axis=-1, keepdims=True))
        return jnp.einsum('hqk,khd->qhd', low(attn_probs), value_block, precision=lax.Precision.HIGHEST)
    blocks = lax.map(jax.checkpoint(one_block), jnp.arange(block_count, dtype=jnp.int32))
    return blocks.reshape(length, HEADS, HEAD_DIM)

def forward(inputs, gain_one, qkv_weight, attn_out_weight, gain_two, in_weight, mlp_out_weight):
    length = inputs.shape[0]
    normed_one = low(layer_norm(inputs, gain_one))
    projected = low_back(jnp.dot(normed_one, qkv_weight, precision=lax.Precision.HIGHEST))
    projected = projected.reshape(length, 3, HEADS, HEAD_DIM)
    positions = jnp.arange(length, dtype=jnp.int32)
    queries = low(rotary(projected[:, 0], positions))
    keys_rot = low(rotary(projected[:, 1], positions))
    values_in = low(projected[:, 2])
    attended = low(low_back(attend(queries, keys_rot, values_in).reshape(length, D)))
    hidden = inputs + low_back(jnp.dot(attended, attn_out_weight, precision=lax.Precision.HIGHEST))
    normed_two = low(layer_norm(hidden, gain_two))
    up_proj = low_back(jnp.dot(normed_two, in_weight, precision=lax.Precision.HIGHEST))
    mixed = low(gelu_exact(up_proj[:, :FF]) * up_proj[:, FF:])
    return hidden + low_back(jnp.dot(mixed, mlp_out_weight, precision=lax.Precision.HIGHEST))

def reference(tokens, norm_gain_one, qkv_weight, attn_out_weight, norm_gain_two, in_weight, mlp_out_weight, cotangent):
    params = (norm_gain_one.astype(jnp.float32), qkv_weight.astype(jnp.float32), attn_out_weight.astype(jnp.float32), norm_gain_two.astype(jnp.float32), in_weight.astype(jnp.float32), mlp_out_weight.astype(jnp.float32))
    token_seqs = tokens.astype(jnp.float32).reshape(SEQS, SEQ_LEN, D)
    cot_seqs = cotangent.astype(jnp.float32).reshape(SEQS, SEQ_LEN, D)

    def scan_step(running, inputs_pair):
        seq_in, seq_cot = inputs_pair
        seq_out, pullback = jax.vjp(forward, seq_in, *params)
        gradients = pullback(seq_cot)
        updated = tuple((total + part for total, part in zip(running, gradients[1:])))
        return (updated, (seq_out, gradients[0]))
    initial = tuple((jnp.zeros_like(param) for param in params))
    totals, (outputs, input_grads) = lax.scan(scan_step, initial, (token_seqs, cot_seqs))
    return (outputs.reshape(TOKENS, D).astype(jnp.bfloat16), input_grads.reshape(TOKENS, D).astype(jnp.bfloat16), totals[0], totals[1], totals[2], totals[3], totals[4], totals[5])
```

```python
from functools import partial

import jax
import jax.numpy as jnp
from jax import lax
from jax.sharding import PartitionSpec as P

HEADS = 12
HEAD_DIM = 64
FF = 1152
HALF_WIN = 64


eps_norm = 1e-05
theta = 10000.0
masked_value = -1e30


def with_halo(x, sides, width):
    for axis, dim in sides:
        peers, length = (lax.axis_size(axis), x.shape[dim])
        up = [(i, (i + 1) % peers) for i in range(peers - 1)]
        down = [(j, i) for i, j in up]
        last = lax.slice_in_dim(x, length - width, length, axis=dim)
        first = lax.slice_in_dim(x, 0, width, axis=dim)
        before = lax.ppermute(last, axis, up)
        after = lax.ppermute(first, axis, down)
        x = jnp.concatenate([before, x, after], axis=dim)
    return x


YAXIS, XAXIS, NEAR, CORE, FAR = "y", "x", "zl", "c", "zh"
PAIRS_A = [(0, 1), (1, 0), (2, 3), (3, 2)]
PAIRS_B = [(0, 3), (3, 0), (1, 2), (2, 1)]
SWAP = [(0, 1), (1, 0)]


def by_core(axis, even, odd):
    return [
        (i * 2 + c, j * 2 + c) for c, pairs in ((0, even), (1, odd)) for i, j in pairs
    ]


def ring_swap(x, axis, first):
    even, odd = (PAIRS_A, PAIRS_B) if first else (PAIRS_B, PAIRS_A)
    if axis == YAXIS:
        pairs = [
            ((i * 4 + k) * 4 + r, (j * 4 + k) * 4 + r)
            for z in range(2)
            for c, group in ((0, even), (1, odd))
            for r in (z * 2 + c,)
            for k in range(4)
            for i, j in group
        ]
        return lax.ppermute(x, (YAXIS, XAXIS, NEAR, CORE), pairs)
    pairs = [
        (i * 4 + z * 2 + c, j * 4 + z * 2 + c)
        for z in range(2)
        for c, group in ((0, even), (1, odd))
        for i, j in group
    ]
    return lax.ppermute(x, (XAXIS, NEAR, CORE), pairs)


def depth_swap(x, first):
    across = [(i, 3 - i) for i in range(4)]
    within = [(i, i ^ 2) for i in range(4)]
    even, odd = (across, within) if first else (within, across)
    pairs = []
    for c, group in ((0, even), (1, odd)):
        for i, j in group:
            pairs.append(((i >> 1) * 4 + c * 2 + (i & 1), (j >> 1) * 4 + c * 2 + (j & 1)))
    return lax.ppermute(x, (NEAR, CORE, FAR), pairs)


def across_halves(x):
    return lax.ppermute(x, (NEAR, FAR), [(i, 3 - i) for i in range(4)])


def core_swap(x):
    return lax.ppermute(x, CORE, SWAP)


def pick(x, index, axis):
    return lax.dynamic_index_in_dim(x, index, axis, keepdims=False)


def ordered(mine, other, index, axis):
    return jnp.where(index == 0, jnp.stack([mine, other], axis), jnp.stack([other, mine], axis))


def add(a, b):
    return (a.astype(jnp.float32) + b.astype(jnp.float32)).astype(jnp.bfloat16)


def whole_rows(own):
    rows, cols = own.shape
    core, half = lax.axis_index(CORE), lax.axis_index(FAR)
    piece = across_halves(pick(own.reshape(2, rows // 2, cols), core, 0))
    missing = ordered(piece, core_swap(piece), core, 0).reshape(rows, cols)
    return ordered(own, missing, half, 0).reshape(2 * rows, cols)


def total_rows(partial):
    rows, cols = partial.shape
    core, half = lax.axis_index(CORE), lax.axis_index(FAR)
    near, xi, yi = lax.axis_index(NEAR), lax.axis_index(XAXIS), lax.axis_index(YAXIS)
    first_bit = lambda i: jnp.where(core == 0, ((i + 1) >> 1) & 1, i >> 1)
    second_bit = lambda i: i & 1
    near = near ^ half
    data = partial.astype(jnp.bfloat16).reshape(2, 2, 2, 2, rows // 16, 2, cols // 2)
    data = jnp.moveaxis(data, 5, 0)
    data = add(pick(data, core, 0), core_swap(pick(data, 1 - core, 0)))
    bit = first_bit(xi)
    data = add(pick(data, bit, 1), ring_swap(pick(data, 1 - bit, 1), XAXIS, True))
    bit = second_bit(xi)
    data = add(pick(data, bit, 1), ring_swap(pick(data, 1 - bit, 1), XAXIS, False))
    data = jnp.where(core == 0, data, jnp.swapaxes(data, 0, 1))
    bit = jnp.where(core == 0, half, near)
    data = add(pick(data, bit, 0), depth_swap(pick(data, 1 - bit, 0), True))
    bit = jnp.where(core == 0, near, half)
    data = add(pick(data, bit, 0), depth_swap(pick(data, 1 - bit, 0), False))
    data = add(data, ring_swap(data, YAXIS, True))
    data = add(data, ring_swap(data, YAXIS, False))
    data = ordered(data, lax.ppermute(data, NEAR, SWAP), near, 0)
    data = ordered(data, ring_swap(data, XAXIS, False), second_bit(xi), 0)
    data = ordered(data, ring_swap(data, XAXIS, True), first_bit(xi), 0)
    data = ordered(data, core_swap(data), core, 4)
    return data.reshape(rows // 2, cols).astype(jnp.float32)


def from_behind(x, axis, by):
    peers = lax.axis_size(axis)
    pairs = [(i, i + by) for i in range(peers) if 0 <= i + by < peers]
    return lax.ppermute(x, axis, pairs)


def whole_gain(own):
    half = lax.axis_index(FAR)
    return ordered(own, across_halves(own), half, 0).reshape(-1)


def gain_total(weight_sum, weight, gain):
    return jnp.sum(weight_sum * weight.astype(jnp.float32), axis=-1) / gain.astype(jnp.float32)


def layer_norm(values, gain):
    row_mean = jnp.mean(values, axis=-1, keepdims=True)
    centred = values - row_mean
    variance = jnp.mean(centred * centred, axis=-1, keepdims=True)
    return centred * lax.rsqrt(variance + eps_norm) * gain


def rotary(values, positions):
    half_dim = values.shape[-1] // 2
    frequency = theta ** (-(jnp.arange(half_dim, dtype=jnp.float32) * 2.0 / values.shape[-1]))
    angles = positions.astype(jnp.float32)[:, None] * frequency[None, :]
    cosine = jnp.concatenate([jnp.cos(angles), jnp.cos(angles)], -1)[:, None, :]
    sine = jnp.concatenate([jnp.sin(angles), jnp.sin(angles)], -1)[:, None, :]
    first_half = values[..., :half_dim]
    second = values[..., half_dim:]
    turned = jnp.concatenate([-second, first_half], -1)
    return values * cosine + turned * sine


def gelu_exact(values):
    return 0.5 * values * (1.0 + lax.erf(values * 0.7071067811865476))


def gated(up_proj, inner):
    return gelu_exact(up_proj[:, :inner]) * up_proj[:, inner:]


def windows(extended_part, blocks, tile):
    tiles = extended_part.reshape(blocks + 1, tile, HEADS, HEAD_DIM)
    return jnp.concatenate([tiles[:-1], tiles[1:]], 1)


def fold_windows(windowed, blocks, tile, width):
    flat = windowed.reshape(blocks, 2 * tile, width)
    first_part = flat[:, :tile].reshape(blocks * tile, width)
    second_part = flat[:, tile:].reshape(blocks * tile, width)
    return jnp.pad(first_part, ((0, tile), (0, 0))) + jnp.pad(second_part, ((tile, 0), (0, 0)))


def local(
    tokens,
    norm_gain_one,
    qkv_weight,
    attn_out_weight,
    norm_gain_two,
    in_weight,
    mlp_out_weight,
    cotangent,
):
    rows, width = tokens.shape
    shard_count = lax.axis_size(FAR)
    seq_len = rows * shard_count
    base_pos = lax.axis_index(FAR) * rows
    positions = base_pos + jnp.arange(rows, dtype=jnp.int32)
    score_scale = HEAD_DIM ** (-0.5)
    tile = 2 * HALF_WIN
    blocks = rows // tile
    full_gain_one = whole_gain(norm_gain_one)
    full_gain_two = whole_gain(norm_gain_two)
    full_qkv, full_attn = whole_rows(qkv_weight), whole_rows(attn_out_weight)
    full_in, full_mlp = whole_rows(in_weight), whole_rows(mlp_out_weight)
    inputs = tokens.astype(jnp.float32)
    normed_one, norm_one_pull = jax.vjp(layer_norm, inputs, full_gain_one.astype(jnp.float32))
    normed_one_b = normed_one.astype(jnp.bfloat16)
    projected = jnp.dot(normed_one_b, full_qkv, preferred_element_type=jnp.float32).reshape(
        rows, 3, HEADS, HEAD_DIM
    )

    def rope_pair(raw_query, raw_key):
        return (rotary(raw_query, positions), rotary(raw_key, positions))

    (rot_query, rot_key), rope_pull = jax.vjp(rope_pair, projected[:, 0], projected[:, 1])
    queries = rot_query.astype(jnp.bfloat16)
    query_tiles = queries.reshape(blocks, tile, HEADS, HEAD_DIM)
    keys_vals = jnp.concatenate(
        [rot_key.reshape(rows, width), projected[:, 2].reshape(rows, width)], 1
    ).astype(jnp.bfloat16)
    extended = with_halo(keys_vals, ((FAR, 0),), HALF_WIN)
    win_keys = windows(extended[:, :width], blocks, tile)
    win_vals = windows(extended[:, width:], blocks, tile)
    local_query = jnp.arange(tile, dtype=jnp.int32)
    local_key = jnp.arange(2 * tile, dtype=jnp.int32)
    block_start = base_pos + jnp.arange(blocks, dtype=jnp.int32) * tile
    key_pos = block_start[:, None] - HALF_WIN + local_key[None, :]
    band = jnp.abs(local_query[:, None] - local_key[None, :] + HALF_WIN) <= HALF_WIN
    inside = (key_pos >= 0) & (key_pos < seq_len)
    allowed = (band[None, :, :] & inside[:, None, :])[:, None]

    def masked_scores():
        raw_scores = (
            jnp.einsum("bqhd,bkhd->bhqk", query_tiles, win_keys, preferred_element_type=jnp.float32)
            * score_scale
        )
        return jnp.where(allowed, raw_scores, masked_value)

    scores = masked_scores()
    top_score = jnp.max(scores, axis=-1, keepdims=True)
    log_total = top_score + jnp.log(jnp.sum(jnp.exp(scores - top_score), axis=-1, keepdims=True))
    probs_b = jnp.exp(scores - log_total).astype(jnp.bfloat16)
    attended = jnp.einsum("bhqk,bkhd->bqhd", probs_b, win_vals, preferred_element_type=jnp.float32)
    attended_b = attended.reshape(rows, width).astype(jnp.bfloat16)
    hidden = inputs + jnp.dot(attended_b, full_attn, preferred_element_type=jnp.float32)
    normed_two, norm_two_pull = jax.vjp(layer_norm, hidden, full_gain_two.astype(jnp.float32))
    normed_two_b = normed_two.astype(jnp.bfloat16)
    up_proj = jnp.dot(normed_two_b, full_in, preferred_element_type=jnp.float32)
    mixed, gate_pull = jax.vjp(partial(gated, inner=FF), up_proj)
    mixed_b = mixed.astype(jnp.bfloat16)
    output = hidden + jnp.dot(mixed_b, full_mlp, preferred_element_type=jnp.float32)
    layer_output = output.astype(jnp.bfloat16)
    back_in, back_mlp, back_qkv, back_attn = full_in, full_mlp, full_qkv, full_attn
    grad_out = cotangent.astype(jnp.float32)
    mlp_out_full = jnp.einsum("tf,td->fd", mixed_b, cotangent, preferred_element_type=jnp.float32)
    d_mixed = jnp.einsum("td,fd->tf", cotangent, back_mlp, preferred_element_type=jnp.float32)
    (d_up,) = gate_pull(d_mixed)
    d_up_b = d_up.astype(jnp.bfloat16)
    in_full = jnp.einsum("td,tf->df", normed_two_b, d_up_b, preferred_element_type=jnp.float32)
    d_normed_two = jnp.einsum("tf,df->td", d_up_b, back_in, preferred_element_type=jnp.float32)
    d_hidden_norm, _ = norm_two_pull(d_normed_two)
    d_hidden = grad_out + d_hidden_norm
    in_sum, mlp_out_sum = total_rows(in_full), total_rows(mlp_out_full)
    d_branch_b = d_hidden.astype(jnp.bfloat16)
    attn_out_full = jnp.einsum(
        "tc,td->cd", attended_b, d_branch_b, preferred_element_type=jnp.float32
    )
    d_attended = jnp.einsum("td,cd->tc", d_branch_b, back_attn, preferred_element_type=jnp.float32)
    d_attended_b = d_attended.astype(jnp.bfloat16).reshape(blocks, tile, HEADS, HEAD_DIM)
    probs = jnp.exp(masked_scores() - log_total)
    d_probs = jnp.einsum(
        "bqhd,bkhd->bhqk", d_attended_b, win_vals, preferred_element_type=jnp.float32
    )
    row_delta = jnp.sum(probs * d_probs, axis=-1, keepdims=True)
    d_scores_b = (probs * (d_probs - row_delta)).astype(jnp.bfloat16)
    d_queries = (
        jnp.einsum("bhqk,bkhd->bqhd", d_scores_b, win_keys, preferred_element_type=jnp.float32)
        * score_scale
    )
    d_queries = d_queries.reshape(rows, HEADS, HEAD_DIM)
    d_win_keys = (
        jnp.einsum("bhqk,bqhd->bkhd", d_scores_b, query_tiles, preferred_element_type=jnp.float32)
        * score_scale
    )
    d_win_vals = jnp.einsum(
        "bhqk,bqhd->bkhd", probs_b, d_attended_b, preferred_element_type=jnp.float32
    )
    d_extended = jnp.concatenate(
        [
            fold_windows(d_win_keys, blocks, tile, width),
            fold_windows(d_win_vals, blocks, tile, width),
        ],
        1,
    )
    from_upper = from_behind(d_extended[:HALF_WIN].astype(jnp.bfloat16), FAR, -1).astype(
        jnp.float32
    )
    from_lower = from_behind(d_extended[rows + HALF_WIN :].astype(jnp.bfloat16), FAR, 1).astype(
        jnp.float32
    )
    d_owned = d_extended[HALF_WIN : HALF_WIN + rows]
    d_owned = (
        d_owned
        + jnp.pad(from_upper, ((rows - HALF_WIN, 0), (0, 0)))
        + jnp.pad(from_lower, ((0, rows - HALF_WIN), (0, 0)))
    )
    d_rot_key = d_owned[:, :width].reshape(rows, HEADS, HEAD_DIM)
    d_raw_value = d_owned[:, width:].reshape(rows, HEADS, HEAD_DIM)
    d_raw_query, d_raw_key = rope_pull((d_queries, d_rot_key))
    d_projected_b = (
        jnp.stack([d_raw_query, d_raw_key, d_raw_value], 1)
        .reshape(rows, 3 * width)
        .astype(jnp.bfloat16)
    )
    qkv_full = jnp.einsum(
        "td,tc->dc", normed_one_b, d_projected_b, preferred_element_type=jnp.float32
    )
    d_normed_one = jnp.einsum(
        "tc,dc->td", d_projected_b, back_qkv, preferred_element_type=jnp.float32
    )
    d_input_norm, _ = norm_one_pull(d_normed_one)
    token_grad = (d_hidden + d_input_norm).astype(jnp.bfloat16)
    attn_out_sum, qkv_sum = total_rows(attn_out_full), total_rows(qkv_full)
    gain_one_sum = gain_total(qkv_sum, qkv_weight, norm_gain_one)
    gain_two_sum = gain_total(in_sum, in_weight, norm_gain_two)
    return (
        layer_output,
        token_grad,
        gain_one_sum,
        qkv_sum,
        attn_out_sum,
        gain_two_sum,
        in_sum,
        mlp_out_sum,
    )


def solution(mesh):
    fine = jax.sharding.Mesh(
        mesh.devices.reshape(4, 4, 2, 2, 2), (YAXIS, XAXIS, NEAR, CORE, FAR)
    )
    every = P((YAXIS, XAXIS, NEAR, CORE, FAR), None)
    return jax.shard_map(
        local,
        mesh=fine,
        in_specs=(every, P(FAR), P(FAR, None), P(FAR, None), P(FAR), P(FAR, None), P(FAR, None), every),
        out_specs=(every, every, P(FAR), P(FAR, None), P(FAR, None), P(FAR), P(FAR, None), P(FAR, None)),
        check_vma=False,
    )
```

```python
import math

import jax
import jax.numpy as jnp
from jax import lax
from jax.experimental import pallas as pl
from jax.experimental.pallas import tpu as pltpu
from jax.sharding import PartitionSpec as P

HEADS = 12
HEAD_DIM = 64
FF = 1152
HALF_WIN = 64
TILE = 2 * HALF_WIN
ROWS = 512
F32, BF16 = jnp.float32, jnp.bfloat16

eps_norm = 1e-05
theta = 10000.0
masked_value = -1e30

YAXIS, XAXIS, NEAR, CORE, FAR = "y", "x", "zl", "c", "zh"
PAIRS_A = [(0, 1), (1, 0), (2, 3), (3, 2)]
PAIRS_B = [(0, 3), (3, 0), (1, 2), (2, 1)]
SWAP = [(0, 1), (1, 0)]


def ring_swap(x, axis, first):
    even, odd = (PAIRS_A, PAIRS_B) if first else (PAIRS_B, PAIRS_A)
    if axis == YAXIS:
        pairs = [
            ((i * 4 + k) * 4 + r, (j * 4 + k) * 4 + r)
            for z in range(2)
            for c, group in ((0, even), (1, odd))
            for r in (z * 2 + c,)
            for k in range(4)
            for i, j in group
        ]
        return lax.ppermute(x, (YAXIS, XAXIS, NEAR, CORE), pairs)
    pairs = [
        (i * 4 + z * 2 + c, j * 4 + z * 2 + c)
        for z in range(2)
        for c, group in ((0, even), (1, odd))
        for i, j in group
    ]
    return lax.ppermute(x, (XAXIS, NEAR, CORE), pairs)


def depth_swap(x, first):
    across = [(i, 3 - i) for i in range(4)]
    within = [(i, i ^ 2) for i in range(4)]
    even, odd = (across, within) if first else (within, across)
    pairs = []
    for c, group in ((0, even), (1, odd)):
        for i, j in group:
            pairs.append(((i >> 1) * 4 + c * 2 + (i & 1), (j >> 1) * 4 + c * 2 + (j & 1)))
    return lax.ppermute(x, (NEAR, CORE, FAR), pairs)


def across_halves(x):
    return lax.ppermute(x, (NEAR, FAR), [(i, 3 - i) for i in range(4)])


def core_swap(x):
    return lax.ppermute(x, CORE, SWAP)


def pick(x, index, axis):
    return lax.dynamic_index_in_dim(x, index, axis, keepdims=False)


def ordered(mine, other, index, axis):
    return jnp.where(index == 0, jnp.stack([mine, other], axis), jnp.stack([other, mine], axis))


def add(a, b):
    return (a.astype(jnp.float32) + b.astype(jnp.float32)).astype(jnp.bfloat16)


def ln_stats(v):
    mean = jnp.mean(v, axis=-1, keepdims=True)
    centred = v - mean
    scale = lax.rsqrt(jnp.mean(centred * centred, axis=-1, keepdims=True) + eps_norm)
    return centred * scale, scale


def ln_back(grad, gain, normal, scale):
    inner = grad * gain
    mean_inner = jnp.mean(inner, axis=-1, keepdims=True)
    mean_cross = jnp.mean(inner * normal, axis=-1, keepdims=True)
    return scale * (inner - mean_inner - normal * mean_cross)


def mm(a, b):
    return jnp.dot(a, b, preferred_element_type=F32)


def mm_nt(a, b):
    return lax.dot_general(a, b, (((1,), (1,)), ((), ())), preferred_element_type=F32)


def mm_tn(a, b):
    return lax.dot_general(a, b, (((0,), (0,)), ((), ())), preferred_element_type=F32)


def rows_loop(rows, chunk, body):
    def step(i, carry):
        body(pl.ds(pl.multiple_of(i * chunk, chunk), chunk))
        return carry

    lax.fori_loop(0, rows // chunk, step, 0)


def place_weight(where_ref, pieces, full, sems, skip=0):
    half, core = where_ref[0], where_ref[1]
    own, mine, others = pieces
    rows = own.shape[0]
    block = rows // 2
    other = (1 - half) * rows
    copies = [pltpu.make_async_copy(own, full.at[pl.ds(pl.multiple_of(half * rows, 32), rows)], sems.at[0])]
    for n, (source, which) in enumerate(((mine, core), (others, 1 - core))):
        place = pl.ds(pl.multiple_of(other + which * block, 32), block)
        copies.append(pltpu.make_async_copy(source.at[pl.ds(skip, block)], full.at[place], sems.at[1 + n]))
    for copy in copies:
        copy.start()
    return copies


def turned(tile, lane):
    return jnp.where(lane, pltpu.roll(tile, 96, 1), pltpu.roll(tile, 32, 1))


def low_lanes(rows, period):
    lanes = lax.broadcasted_iota(jnp.int32, (rows, 128), 1)
    return (lanes % period) < period // 2


def qkv_kernel(where_ref, x_ref, beside_ref, gain_ref, cos_ref, sin_ref, own, first, second,
               normed_out, query_out, key_out, value_out, full, sems):
    copies = place_weight(where_ref, (own, first, second), full, sems)
    normed, query_ref, key_ref, value_ref = (out.ref for out in (normed_out, query_out, key_out, value_out))
    gain, x_ref, beside_ref = gain_ref()[...], x_ref(), beside_ref()

    def main(rows):
        normal, _ = ln_stats(x_ref[rows, :].astype(F32))
        normed[rows, :] = (normal * gain).astype(BF16)

    rows_loop(ROWS, 128, main)
    normal, _ = ln_stats(beside_ref[...].astype(F32))
    normed[ROWS:, :] = (normal * gain).astype(BF16)
    normed_out.send()
    for copy in copies:
        copy.wait()
    cos_ref, sin_ref = cos_ref(), sin_ref()
    lane = low_lanes(ROWS + HALF_WIN, HEAD_DIM)
    for j in range(9):
        cols = slice(j * 256, (j + 1) * 256)
        proj = mm(normed[...], full[:, cols])
        for side in range(2):
            tile = proj[:, side * 128 : (side + 1) * 128]
            if j < 6:
                tile = tile * cos_ref[...] + turned(tile, lane) * sin_ref[...]
            place = slice((j % 3) * 256 + side * 128, (j % 3) * 256 + (side + 1) * 128)
            if j < 3:
                query_ref[:, place] = (tile[:ROWS] * 0.125).astype(BF16)
            else:
                out_ref = key_ref if j < 6 else value_ref
                edge = tile[ROWS:].astype(BF16)
                out_ref[HALF_WIN : HALF_WIN + ROWS, place] = tile[:ROWS].astype(BF16)
                out_ref[:HALF_WIN, place] = edge
                out_ref[HALF_WIN + ROWS :, place] = edge
        if j == 2:
            query_out.send()
        if j == 5:
            key_out.send()


def attend_kernel(where_ref, q_ref, k_ref, v_ref, x_ref, own, first, second,
                  att_out, prob_out, hidden_out, full, sems):
    copies = place_weight(where_ref, (own, first, second), full, sems)
    att_ref, prob_ref, hidden_ref = att_out.ref, prob_out.ref, hidden_out.ref
    q_ref, k_ref, v_ref = q_ref(), k_ref(), v_ref()
    half = where_ref[0]
    low_q, low_k = low_lanes(TILE, 128), low_lanes(2 * TILE, 128)
    row = lax.broadcasted_iota(jnp.int32, (2 * TILE, 2 * TILE), 0) % TILE
    col = lax.broadcasted_iota(jnp.int32, (2 * TILE, 2 * TILE), 1)
    band = (col >= row) & (col <= row + 2 * HALF_WIN)

    def tile_step(t, carry):
        begin = jnp.where((half == 0) & (t == 0), HALF_WIN, 0)
        end = jnp.where((half == 1) & (t == ROWS // TILE - 1), 2 * TILE - HALF_WIN, 2 * TILE)
        allowed = band & (col >= begin) & (col < end)
        rows = pl.ds(pl.multiple_of(t * TILE, TILE), TILE)
        span = pl.ds(pl.multiple_of(t * TILE, TILE), 2 * TILE)
        for pair in range(HEADS // 2):
            lanes = slice(pair * 128, (pair + 1) * 128)
            q = q_ref[rows, lanes]
            zero = jnp.zeros_like(q)
            stacked = jnp.concatenate([jnp.where(low_q, q, zero), jnp.where(low_q, zero, q)], 0)
            scores = jnp.where(allowed, mm_nt(stacked, k_ref[span, lanes]), masked_value)
            raised = jnp.exp(scores - jnp.max(scores, axis=-1, keepdims=True))
            probs = (raised / jnp.sum(raised, axis=-1, keepdims=True)).astype(BF16)
            prob_ref[t, pair] = probs
            v = v_ref[span, lanes]
            none = jnp.zeros_like(v)
            att_ref[rows, lanes] = mm(
                jnp.concatenate([probs[:TILE], probs[TILE:]], 1),
                jnp.concatenate([jnp.where(low_k, v, none), jnp.where(low_k, none, v)], 0),
            ).astype(BF16)
        return carry

    lax.fori_loop(0, ROWS // TILE, tile_step, 0)
    prob_out.send()
    att_out.send()
    x_ref = x_ref()
    for copy in copies:
        copy.wait()
    for j in range(3):
        cols = slice(j * 256, (j + 1) * 256)
        hidden_ref[:, cols] = x_ref[:, cols].astype(F32) + mm(att_ref[...], full[:, cols])


def mlp_kernel(where_ref, hidden_ref, gain_ref, cot_ref, in_own, in_first, in_second,
               out_own, out_first, out_second,
               up_out, send_out, keep_out, layer_out, w_in, w_out, normed, mixed, act_s, gate_s, dmix_s, sems):
    in_copies = place_weight(where_ref, (in_own, in_first, in_second), w_in, sems.at[0])
    out_copies = place_weight(where_ref, (out_own, out_first, out_second), w_out, sems.at[1], 192)
    core = where_ref[1]
    d_up, layer_ref = up_out.ref, layer_out.ref
    hidden_ref, gain = hidden_ref(), gain_ref()[...]

    def normalize(rows):
        normal, _ = ln_stats(hidden_ref[rows, :])
        normed[rows, :] = (normal * gain).astype(BF16)

    rows_loop(ROWS, 128, normalize)
    cot_ref = cot_ref()
    for copy in in_copies + out_copies:
        copy.wait()
    for j in range(3):
        cols = slice(j * 384, (j + 1) * 384)
        gates = slice(FF + j * 384, FF + (j + 1) * 384)
        act_s[...] = mm(normed[...], w_in[:, cols])
        gate_s[...] = mm(normed[...], w_in[:, gates])
        dmix_s[...] = mm_nt(cot_ref[...], w_out[cols, :])

        def gate(rows):
            act, gated_by, d_mixed = act_s[rows, :], gate_s[rows, :], dmix_s[rows, :]
            cumulative = 0.5 * (1.0 + lax.erf(act * 0.7071067811865476))
            density = jnp.exp(-0.5 * act * act) * 0.3989422804014327
            curved = act * cumulative
            mixed[rows, cols] = (curved * gated_by).astype(BF16)
            d_up[rows, cols] = (d_mixed * gated_by * (cumulative + act * density)).astype(BF16)
            d_up[rows, gates] = (d_mixed * curved).astype(BF16)

        rows_loop(ROWS, 128, gate)
    up_out.send()
    for out, which in ((send_out, 1 - core), (keep_out, core)):
        for j in range(3):
            cols = pl.ds(pl.multiple_of(which * 1152 + j * 384, 128), 384)
            grad = mm_tn(normed[...], d_up[:, cols]).astype(BF16)
            out.ref[:, :, j * 96 : (j + 1) * 96] = grad.reshape(2, 4, 96, 384)
        cols = pl.ds(pl.multiple_of(which * 384, 128), 384)
        grad = mm_tn(mixed[...], cot_ref[:, cols]).astype(BF16)
        out.ref[:, :, 288:] = grad.reshape(2, 4, 144, 384)
        out.send()
    for j in range(3):
        cols = slice(j * 256, (j + 1) * 256)
        layer_ref[:, cols] = (hidden_ref[:, cols] + mm(mixed[...], w_out[:, cols])).astype(BF16)


def mlp_back_kernel(where_ref, up_ref, hidden_ref, cot_ref, gain_ref, in_own, in_first, in_second,
                    dhid_out, w_in, dnorm_s, sems):
    copies = place_weight(where_ref, (in_own, in_first, in_second), w_in, sems)
    d_up = up_ref()
    for copy in copies:
        copy.wait()
    for j in range(3):
        cols = slice(j * 256, (j + 1) * 256)
        dnorm_s[:, cols] = mm_nt(d_up[...], w_in[cols, :])
    hidden_ref, cot_ref, gain = hidden_ref(), cot_ref(), gain_ref()[...]

    def back(rows):
        normal, scale = ln_stats(hidden_ref[rows, :])
        dhid_out.ref[rows, :] = cot_ref[rows, :].astype(F32) + ln_back(dnorm_s[rows, :], gain, normal, scale)

    rows_loop(ROWS, 128, back)


def attend_back_kernel(where_ref, dhid_ref, q_ref, k_ref, v_ref, prob_ref, cos_ref, sin_ref, att_ref, normed_ref,
                       own, first, second, dproj_out, edge_out, send_out, keep_out,
                       full, branch, datt, dkey, dvalue, grads_s, sems):
    copies = place_weight(where_ref, (own, first, second), full, sems)
    half, core = where_ref[0], where_ref[1]
    dproj_ref, edge_ref = dproj_out.ref, edge_out.ref
    dkey[...] = jnp.zeros_like(dkey)
    dvalue[...] = jnp.zeros_like(dvalue)
    for copy in copies:
        copy.wait()
    branch[...] = dhid_ref()[...].astype(BF16)
    for j in range(3):
        cols = slice(j * 256, (j + 1) * 256)
        datt[:, cols] = mm_nt(branch[...], full[cols, :]).astype(BF16)
    q_ref, k_ref, v_ref, prob_ref, cos_ref, sin_ref = (
        ref() for ref in (q_ref, k_ref, v_ref, prob_ref, cos_ref, sin_ref)
    )
    low_q, low_k = low_lanes(TILE, 128), low_lanes(2 * TILE, 128)
    turn_q = low_lanes(TILE, HEAD_DIM)

    def split(tile, low, axis=0):
        none = jnp.zeros_like(tile)
        return jnp.concatenate([jnp.where(low, tile, none), jnp.where(low, none, tile)], axis)

    def tile_step(t, carry):
        rows = pl.ds(pl.multiple_of(t * TILE, TILE), TILE)
        span = pl.ds(pl.multiple_of(t * TILE, TILE), 2 * TILE)
        cos, sin = cos_ref[rows, :], sin_ref[rows, :]
        for pair in range(HEADS // 2):
            lanes = slice(pair * 128, (pair + 1) * 128)
            grads = split(datt[rows, lanes], low_q)
            probs_b = prob_ref[t, pair]
            probs = probs_b.astype(F32)
            d_probs = mm_nt(grads, v_ref[span, lanes])
            delta = jnp.sum(probs * d_probs, axis=-1, keepdims=True)
            d_scores = (probs * (d_probs - delta)).astype(BF16)
            d_query = 0.125 * mm(
                jnp.concatenate([d_scores[:TILE], d_scores[TILE:]], 1), split(k_ref[span, lanes], low_k)
            )
            dproj_ref[rows, lanes] = (d_query * cos - turned(d_query, turn_q) * sin).astype(BF16)
            dkey[span, lanes] += mm_tn(d_scores, split(q_ref[rows, lanes], low_q))
            dvalue[span, lanes] += mm_tn(probs_b, grads)
        return carry

    lax.fori_loop(0, ROWS // TILE, tile_step, 0)
    turn_k = low_lanes(ROWS, HEAD_DIM)
    turn_e = low_lanes(HALF_WIN, HEAD_DIM)
    edge = pl.ds(pl.multiple_of((1 - half) * (ROWS + HALF_WIN), HALF_WIN), HALF_WIN)
    for pair in range(HEADS // 2):
        lanes = slice(pair * 128, (pair + 1) * 128)
        tile = dkey[HALF_WIN : HALF_WIN + ROWS, lanes]
        dproj_ref[:, 768 + pair * 128 : 768 + (pair + 1) * 128] = (
            tile * cos_ref[:ROWS] - turned(tile, turn_k) * sin_ref[:ROWS]
        ).astype(BF16)
        dproj_ref[:, 1536 + pair * 128 : 1536 + (pair + 1) * 128] = dvalue[
            HALF_WIN : HALF_WIN + ROWS, lanes
        ].astype(BF16)
        tile = dkey[edge, lanes]
        edge_ref[:, lanes] = (tile * cos_ref[ROWS:] - turned(tile, turn_e) * sin_ref[ROWS:]).astype(BF16)
        edge_ref[:, 768 + pair * 128 : 768 + (pair + 1) * 128] = dvalue[edge, lanes].astype(BF16)
    edge_out.send()
    dproj_out.send()
    normed_ref, att_ref = normed_ref(), att_ref()
    grads_s[:ROWS, :] = dproj_ref[...]
    grads_s[ROWS:, :768] = jnp.zeros((HALF_WIN, 768), BF16)
    grads_s[ROWS:, 768:] = edge_ref[...]
    for out, which in ((send_out, 1 - core), (keep_out, core)):
        for j in range(3):
            cols = pl.ds(pl.multiple_of(which * 1152 + j * 384, 128), 384)
            grad = mm_tn(normed_ref[...], grads_s[:, cols]).astype(BF16)
            out.ref[:, :, j * 96 : (j + 1) * 96] = grad.reshape(2, 4, 96, 384)
        cols = pl.ds(pl.multiple_of(which * 384, 128), 384)
        grad = mm_tn(att_ref[...], branch[:, cols]).astype(BF16)
        out.ref[:, :, 288:] = grad.reshape(2, 4, 96, 384)
        out.send()


def token_grad_kernel(where_ref, x_ref, gain_ref, dproj_ref, edge_ref, dhid_ref, own, first, second,
                      out, full, dnorm, sems):
    copies = place_weight(where_ref, (own, first, second), full, sems)
    grads, edge_ref = dproj_ref(), edge_ref()
    edge = pl.ds(pl.multiple_of((1 - where_ref[0]) * (ROWS - HALF_WIN), HALF_WIN), HALF_WIN)
    grads[edge, 768:] = (grads[edge, 768:].astype(F32) + edge_ref[...].astype(F32)).astype(BF16)
    for copy in copies:
        copy.wait()
    for j in range(3):
        cols = slice(j * 256, (j + 1) * 256)
        dnorm[:, cols] = mm_nt(grads[...], full[cols, :])

    gain, x_ref, dhid_ref = gain_ref()[...], x_ref(), dhid_ref()

    def back(rows):
        normal, scale = ln_stats(x_ref[rows, :].astype(F32))
        out.ref[rows, :] = (dhid_ref[rows, :] + ln_back(dnorm[rows, :], gain, normal, scale)).astype(BF16)

    rows_loop(ROWS, 128, back)


def finish_kernel(where_ref, mine, other, weight, gain, wide_out, narrow_out, gain_out):
    core = where_ref[1]
    wide_ref, narrow_ref = wide_out.ref, narrow_out.ref
    rows = narrow_ref.shape[0]
    for staged, which in ((mine, core), (other, 1 - core)):
        source = staged()
        for j in range(3):
            cols = pl.ds(pl.multiple_of(which * 1152 + j * 384, 128), 384)
            wide_ref[:, cols] = source[:, j * 96 : (j + 1) * 96].reshape(384, 384).astype(F32)
        cols = pl.ds(pl.multiple_of(which * 384, 128), 384)
        narrow_ref[:, cols] = source[:, 288:].reshape(rows, 384).astype(F32)
    wide_out.send()
    narrow_out.send()
    gain_rows(wide_ref, weight(), gain(), gain_out.ref)


def gain_rows(grad_ref, weight, gain, gain_ref):
    for n in range(3):
        rows = slice(n * 128, (n + 1) * 128)
        total = jnp.sum(grad_ref[rows, :] * weight[rows, :].astype(F32), axis=-1, keepdims=True)
        gain_ref[:, rows] = jnp.broadcast_to(total, (128, 128)).T[:1] / gain[:, rows].astype(F32)


class Staged:
    def __init__(self, source, ref, sem):
        self.ref, self.copy, self.there = ref, pltpu.make_async_copy(source, ref, sem), False
        self.copy.start()

    def __call__(self):
        if not self.there:
            self.copy.wait()
            self.there = True
        return self.ref


class Result:
    def __init__(self, ref, target, sem):
        self.ref, self.copy, self.sent = ref, pltpu.make_async_copy(ref, target, sem), False

    def send(self):
        if not self.sent:
            self.copy.start()
            self.sent = True


def run(kernel, ins, outs, scratch, flops):
    staged = [a for a, kind in ins if kind == "v"]
    spaces = {"s": pltpu.SMEM, "h": pl.ANY, "v": pl.ANY}
    moved = sum(a.size * a.dtype.itemsize for a, _ in ins) + sum(
        math.prod(shape) * jnp.dtype(dtype).itemsize for shape, dtype in outs
    )

    def body(*refs):
        given, refs = refs[: len(ins)], refs[len(ins) :]
        targets, refs = refs[: len(outs)], refs[len(outs) :]
        places, refs = refs[: len(staged)], refs[len(staged) :]
        ready, refs = refs[: len(outs)], refs[len(outs) :]
        in_sems, out_sems, *rest = refs
        taken, n = [], 0
        for ref, (_, kind) in zip(given, ins):
            if kind == "v":
                ref = Staged(ref, places[n], in_sems.at[n])
                n += 1
            taken.append(ref)
        results = [Result(r, t, out_sems.at[k]) for k, (r, t) in enumerate(zip(ready, targets))]
        kernel(*taken, *results, *rest)
        for ref in taken:
            if isinstance(ref, Staged):
                ref()
        for result in results:
            result.send()
        for result in results:
            result.copy.wait()

    dma = pltpu.SemaphoreType.DMA
    return pl.pallas_call(
        body,
        in_specs=[pl.BlockSpec(memory_space=spaces[kind]) for _, kind in ins],
        out_specs=[pl.BlockSpec(memory_space=pl.ANY) for _ in outs],
        out_shape=[jax.ShapeDtypeStruct(shape, dtype) for shape, dtype in outs],
        scratch_shapes=[pltpu.VMEM(a.shape, a.dtype) for a in staged]
        + [pltpu.VMEM(shape, dtype) for shape, dtype in outs]
        + [dma((len(staged),)), dma((len(outs),))]
        + scratch,
        compiler_params=pltpu.CompilerParams(vmem_limit_bytes=60 * 1024 * 1024),
        cost_estimate=pl.CostEstimate(flops=int(flops), bytes_accessed=int(moved), transcendentals=0),
    )(*[a for a, _ in ins])


def together(*arrays):
    return lax.optimization_barrier(arrays)


def quarter_of(own):
    rows, cols = own.shape
    return pick(own.reshape(2, rows // 2, cols), lax.axis_index(CORE), 0)


def total_rows(send, keep, shape, first_axis, last_axis):
    core, half = lax.axis_index(CORE), lax.axis_index(FAR)
    near, place = lax.axis_index(NEAR) ^ half, lax.axis_index(first_axis)
    first_bit = jnp.where(core == 0, ((place + 1) >> 1) & 1, place >> 1)
    second_bit = place & 1
    send = yield send
    keep, come = keep.reshape(shape), core_swap(send).reshape(shape)
    for bit, first in ((first_bit, True), (second_bit, False)):
        send = yield add(pick(keep, 1 - bit, 1), pick(come, 1 - bit, 1))
        keep, come = add(pick(keep, bit, 1), pick(come, bit, 1)), ring_swap(send, first_axis, first)
    keep, come = (a.reshape((4,) + shape[4:]) for a in (keep, come))

    def two(which_half, which_near):
        index = [jnp.where(core == 0, which_half * 2 + i, i * 2 + which_near) for i in range(2)]
        return jnp.stack([add(pick(keep, i, 0), pick(come, i, 0)) for i in index])

    send = yield two(1 - half, 1 - near)
    keep, come = two(half, near), depth_swap(send, True)
    bit = jnp.where(core == 0, near, half)
    send = yield add(pick(keep, 1 - bit, 0), pick(come, 1 - bit, 0))
    keep, come = add(pick(keep, bit, 0), pick(come, bit, 0)), depth_swap(send, False)
    for first in (True, False):
        send = yield add(keep, come)
        keep, come = send, ring_swap(send, last_axis, first)
    send = yield add(keep, come)
    send = yield ordered(send, lax.ppermute(send, NEAR, SWAP), near, 0)
    send = yield ordered(send, ring_swap(send, first_axis, False), second_bit, 0)
    send = yield ordered(send, ring_swap(send, first_axis, True), first_bit, 0)
    yield send, core_swap(send)


def local(tokens, norm_gain_one, qkv_weight, attn_out_weight, norm_gain_two, in_weight, mlp_out_weight, cotangent):
    core, half = lax.axis_index(CORE), lax.axis_index(FAR)
    where = jnp.stack([half, core]).astype(jnp.int32)
    quarter = across_halves(quarter_of(qkv_weight))
    edge = jnp.where(half == 0, tokens[ROWS - HALF_WIN :], tokens[:HALF_WIN])
    gains = jnp.pad(jnp.stack([norm_gain_one, norm_gain_two]), ((0, 14), (0, 384)))
    beside = lax.ppermute(jnp.concatenate([edge, gains], 0), FAR, SWAP)
    quarter, narrow_own, beside = together(
        quarter, jnp.concatenate([quarter_of(attn_out_weight), quarter_of(mlp_out_weight)], 0), beside
    )
    narrow_quarter = across_halves(narrow_own)
    qkv = (qkv_weight, quarter, core_swap(quarter))
    fetched = beside[HALF_WIN:, :384]
    beside = beside[:HALF_WIN]
    gain_one = ordered(norm_gain_one, fetched[0], half, 0).reshape(1, 768).astype(F32)
    gain_two = ordered(norm_gain_two, fetched[1], half, 0).reshape(1, 768).astype(F32)
    index = jnp.arange(ROWS + HALF_WIN, dtype=jnp.int32)
    position = jnp.where(index < ROWS, half * ROWS + index, jnp.where(half == 0, index, index - HALF_WIN))
    lane = jnp.arange(128, dtype=jnp.int32)
    frequency = theta ** (-((lane % 32).astype(F32) * 2.0 / HEAD_DIM))
    angles = position.astype(F32)[:, None] * frequency[None, :]
    cosine = jnp.cos(angles)
    sine = jnp.where((lane % HEAD_DIM) < HEAD_DIM // 2, -1.0, 1.0) * jnp.sin(angles)

    h = lambda arrays: [(a, "h") for a in arrays]
    v = lambda *arrays: [(a, "v") for a in arrays]
    s = [(where, "s")]
    dma = pltpu.SemaphoreType.DMA
    wide, narrow, tall = pltpu.VMEM((768, 2304), BF16), pltpu.VMEM((768, 768), BF16), pltpu.VMEM((1152, 768), BF16)
    normed, query, key, value = run(
        qkv_kernel, s + v(tokens, beside, gain_one, cosine, sine) + h(qkv),
        [((ROWS + HALF_WIN, 768), BF16), ((ROWS, 768), BF16), ((640, 768), BF16), ((640, 768), BF16)],
        [wide, dma((3,))], 2 * 576 * 768 * 2304,
    )
    query, narrow_quarter, in_own = together(query, narrow_quarter, quarter_of(in_weight))
    in_quarter = across_halves(in_own)
    swapped = core_swap(narrow_quarter)
    attn_out, w_out = (attn_out_weight, narrow_quarter, swapped), (mlp_out_weight, narrow_quarter, swapped)
    attended, probs, hidden = run(
        attend_kernel, s + v(query, key, value, tokens) + h(attn_out),
        [((ROWS, 768), BF16), ((4, 6, 256, 256), BF16), ((ROWS, 768), F32)],
        [narrow, dma((3,))], 2 * 512 * 768 * (768 + 1024),
    )
    hidden, in_quarter = together(hidden, in_quarter)
    w_in = (in_weight, in_quarter, core_swap(in_quarter))
    d_up, send, keep, layer_output = run(
        mlp_kernel, s + v(hidden, gain_two, cotangent) + h(w_in) + h(w_out),
        [((ROWS, 2 * FF), BF16), ((2, 4, 432, 384), BF16), ((2, 4, 432, 384), BF16), ((ROWS, 768), BF16)],
        [wide, tall, pltpu.VMEM((ROWS, 768), BF16), pltpu.VMEM((ROWS, FF), BF16),
         pltpu.VMEM((ROWS, 384), F32), pltpu.VMEM((ROWS, 384), F32), pltpu.VMEM((ROWS, 384), F32), dma((2, 3))],
        2 * 512 * 768 * 5800,
    )
    early = total_rows(send, keep, (2, 2, 2, 2, 216, 384), YAXIS, XAXIS)
    early_next = early.send(early.send(None))
    (d_hidden,) = run(
        mlp_back_kernel, s + v(d_up, hidden, cotangent, gain_two) + h(w_in),
        [((ROWS, 768), F32)], [wide, pltpu.VMEM((ROWS, 768), F32), dma((3,))], 2 * 512 * 768 * 2304,
    )
    early_sent, d_hidden = together(early_next, d_hidden)
    early_next = early.send(early_sent)
    d_projected, edge_grad, send, keep = run(
        attend_back_kernel,
        s + v(d_hidden, query, key, value, probs, cosine, sine, attended, normed) + h(attn_out),
        [((ROWS, 2304), BF16), ((HALF_WIN, 1536), BF16), ((2, 4, 384, 384), BF16), ((2, 4, 384, 384), BF16)],
        [narrow, pltpu.VMEM((ROWS, 768), BF16), pltpu.VMEM((ROWS, 768), BF16), pltpu.VMEM((640, 768), F32),
         pltpu.VMEM((640, 768), F32), pltpu.VMEM((ROWS + HALF_WIN, 2304), BF16), dma((3,))],
        2 * 512 * 768 * (768 + 2048 + 2304 + 768),
    )
    late = total_rows(send, keep, (2, 2, 2, 2, 192, 384), XAXIS, YAXIS)
    late_sent, early_sent = together(late.send(None), early_next)
    edge_grad = lax.ppermute(edge_grad, FAR, SWAP)
    late_next, early_next = late.send(late_sent), early.send(early_sent)
    late_sent, early_sent, edge_grad = together(late_next, early_next, edge_grad)
    (token_grad,) = run(
        token_grad_kernel, s + v(tokens, gain_one, d_projected, edge_grad, d_hidden) + h(qkv),
        [((ROWS, 768), BF16)],
        [wide, pltpu.VMEM((ROWS, 768), F32), dma((3,))], 2 * 512 * 768 * 2304,
    )
    late_next, early_next = late.send(late_sent), early.send(early_sent)
    late_next, early_next, token_grad = together(late_next, early_next, token_grad)
    while not isinstance(early_next, tuple):
        early_next = early.send(early_next)

    def finish(pair, weight, gain, rows):
        return run(
            finish_kernel,
            s + v(*(a.reshape(4, -1, 384) for a in pair), weight, gain.reshape(1, 384)),
            [((384, 2304), F32), ((rows, 768), F32), ((1, 384), F32)], [], 0,
        )

    in_sum, mlp_out_sum, gain_two_sum = finish(early_next, in_weight, norm_gain_two, 576)
    for _ in range(8):
        late_next = late.send(late_next)
    late_next, in_sum = together(late_next, in_sum)
    late_next = late.send(late_next)
    qkv_sum, attn_out_sum, gain_one_sum = finish(late_next, qkv_weight, norm_gain_one, 384)
    return (
        layer_output,
        token_grad,
        gain_one_sum.reshape(384),
        qkv_sum,
        attn_out_sum,
        gain_two_sum.reshape(384),
        in_sum,
        mlp_out_sum,
    )


def solution(mesh):
    fine = jax.sharding.Mesh(
        mesh.devices.reshape(4, 4, 2, 2, 2), (YAXIS, XAXIS, NEAR, CORE, FAR)
    )
    every = P((YAXIS, XAXIS, NEAR, CORE, FAR), None)
    return jax.shard_map(
        local,
        mesh=fine,
        in_specs=(every, P(FAR), P(FAR, None), P(FAR, None), P(FAR), P(FAR, None), P(FAR, None), every),
        out_specs=(every, every, P(FAR), P(FAR, None), P(FAR, None), P(FAR), P(FAR, None), P(FAR, None)),
        check_vma=False,
    )
```

```python
import math

import jax
import jax.numpy as jnp
from jax import lax
from jax.experimental import pallas as pl
from jax.experimental.pallas import tpu as pltpu
from jax.sharding import PartitionSpec as P

HEADS = 12
HEAD_DIM = 64
FF = 1152
HALF_WIN = 64
TILE = 2 * HALF_WIN
ROWS = 512
F32, BF16 = jnp.float32, jnp.bfloat16

eps_norm = 1e-05
theta = 10000.0
masked_value = -1e30

YAXIS, XAXIS, NEAR, CORE, FAR = "y", "x", "zl", "c", "zh"
PAIRS_A = [(0, 1), (1, 0), (2, 3), (3, 2)]
PAIRS_B = [(0, 3), (3, 0), (1, 2), (2, 1)]
SWAP = [(0, 1), (1, 0)]


def ring_swap(x, axis, first):
    even, odd = (PAIRS_A, PAIRS_B) if first else (PAIRS_B, PAIRS_A)
    if axis == YAXIS:
        pairs = [
            ((i * 4 + k) * 4 + r, (j * 4 + k) * 4 + r)
            for z in range(2)
            for c, group in ((0, even), (1, odd))
            for r in (z * 2 + c,)
            for k in range(4)
            for i, j in group
        ]
        return lax.ppermute(x, (YAXIS, XAXIS, NEAR, CORE), pairs)
    pairs = [
        (i * 4 + z * 2 + c, j * 4 + z * 2 + c)
        for z in range(2)
        for c, group in ((0, even), (1, odd))
        for i, j in group
    ]
    return lax.ppermute(x, (XAXIS, NEAR, CORE), pairs)


def depth_swap(x, first):
    across = [(i, 3 - i) for i in range(4)]
    within = [(i, i ^ 2) for i in range(4)]
    even, odd = (across, within) if first else (within, across)
    pairs = []
    for c, group in ((0, even), (1, odd)):
        for i, j in group:
            pairs.append(((i >> 1) * 4 + c * 2 + (i & 1), (j >> 1) * 4 + c * 2 + (j & 1)))
    return lax.ppermute(x, (NEAR, CORE, FAR), pairs)


def across_halves(x):
    return lax.ppermute(x, (NEAR, FAR), [(i, 3 - i) for i in range(4)])


def core_swap(x):
    return lax.ppermute(x, CORE, SWAP)


def pick(x, index, axis):
    return lax.dynamic_index_in_dim(x, index, axis, keepdims=False)


def ordered(mine, other, index, axis):
    return jnp.where(index == 0, jnp.stack([mine, other], axis), jnp.stack([other, mine], axis))


def add(a, b):
    return (a.astype(jnp.float32) + b.astype(jnp.float32)).astype(jnp.bfloat16)


def ln_stats(v):
    mean = jnp.mean(v, axis=-1, keepdims=True)
    centred = v - mean
    scale = lax.rsqrt(jnp.mean(centred * centred, axis=-1, keepdims=True) + eps_norm)
    return centred * scale, scale


def ln_back(grad, gain, normal, scale):
    inner = grad * gain
    mean_inner = jnp.mean(inner, axis=-1, keepdims=True)
    mean_cross = jnp.mean(inner * normal, axis=-1, keepdims=True)
    return scale * (inner - mean_inner - normal * mean_cross)


def mm(a, b):
    return jnp.dot(a, b, preferred_element_type=F32)


def mm_nt(a, b):
    return lax.dot_general(a, b, (((1,), (1,)), ((), ())), preferred_element_type=F32)


def mm_tn(a, b):
    return lax.dot_general(a, b, (((0,), (0,)), ((), ())), preferred_element_type=F32)


def rows_loop(rows, chunk, body):
    def step(i, carry):
        body(pl.ds(pl.multiple_of(i * chunk, chunk), chunk))
        return carry

    lax.fori_loop(0, rows // chunk, step, 0)


def place_weight(where_ref, pieces, full, sems, skip=0, parts=1):
    half, core = where_ref[0], where_ref[1]
    own, mine, others = pieces
    rows, cols = own.shape[0], own.shape[1] // parts
    block = rows // 4
    other = (1 - half) * rows
    copies = [pltpu.make_async_copy(own, full.at[pl.ds(pl.multiple_of(half * rows, 16), rows)], sems.at[0])]
    for source, which in ((mine, core), (others, 1 - core)):
        for b in range(2):
            place = pl.ds(pl.multiple_of(other + (which * 2 + b) * block, 16), block)
            for j in range(parts):
                copies.append(
                    pltpu.make_async_copy(
                        source.at[b, pl.ds(skip + j * block, block)],
                        full.at[place, pl.ds(j * cols, cols)],
                        sems.at[len(copies)],
                    )
                )
    for copy in copies:
        copy.start()
    return copies


def turned(tile, lane):
    return jnp.where(lane, pltpu.roll(tile, 96, 1), pltpu.roll(tile, 32, 1))


def low_lanes(rows, period):
    lanes = lax.broadcasted_iota(jnp.int32, (rows, 128), 1)
    return (lanes % period) < period // 2


def qkv_kernel(where_ref, x_ref, beside_ref, gain_ref, cos_ref, sin_ref, own, first, second,
               normed_out, query_out, key_out, value_out, full, sems):
    copies = place_weight(where_ref, (own, first, second), full, sems)
    normed, query_ref, key_ref, value_ref = (out.ref for out in (normed_out, query_out, key_out, value_out))
    gain, x_ref, beside_ref = gain_ref()[...], x_ref(), beside_ref()

    def main(rows):
        normal, _ = ln_stats(x_ref[rows, :].astype(F32))
        normed[rows, :] = (normal * gain).astype(BF16)

    rows_loop(ROWS, 128, main)
    normal, _ = ln_stats(beside_ref[...].astype(F32))
    normed[ROWS:, :] = (normal * gain).astype(BF16)
    normed_out.send()
    for copy in copies:
        copy.wait()
    cos_ref, sin_ref = cos_ref(), sin_ref()
    lane = low_lanes(ROWS + HALF_WIN, HEAD_DIM)
    for j in range(9):
        cols = slice(j * 256, (j + 1) * 256)
        proj = mm(normed[...], full[:, cols])
        for side in range(2):
            tile = proj[:, side * 128 : (side + 1) * 128]
            if j < 6:
                tile = tile * cos_ref[...] + turned(tile, lane) * sin_ref[...]
            place = slice((j % 3) * 256 + side * 128, (j % 3) * 256 + (side + 1) * 128)
            if j < 3:
                query_ref[:, place] = (tile[:ROWS] * 0.125).astype(BF16)
            else:
                out_ref = key_ref if j < 6 else value_ref
                edge = tile[ROWS:].astype(BF16)
                out_ref[HALF_WIN : HALF_WIN + ROWS, place] = tile[:ROWS].astype(BF16)
                out_ref[:HALF_WIN, place] = edge
                out_ref[HALF_WIN + ROWS :, place] = edge
        if j == 2:
            query_out.send()
        if j == 5:
            key_out.send()


def attend_kernel(where_ref, q_ref, k_ref, v_ref, att_out, prob_out):
    att_ref, prob_ref = att_out.ref, prob_out.ref
    q_ref, k_ref, v_ref = q_ref(), k_ref(), v_ref()
    half = where_ref[0]
    low_q, low_k = low_lanes(TILE, 128), low_lanes(2 * TILE, 128)
    row = lax.broadcasted_iota(jnp.int32, (2 * TILE, 2 * TILE), 0) % TILE
    col = lax.broadcasted_iota(jnp.int32, (2 * TILE, 2 * TILE), 1)
    band = (col >= row) & (col <= row + 2 * HALF_WIN)

    def tile_step(t, carry):
        begin = jnp.where((half == 0) & (t == 0), HALF_WIN, 0)
        end = jnp.where((half == 1) & (t == ROWS // TILE - 1), 2 * TILE - HALF_WIN, 2 * TILE)
        allowed = band & (col >= begin) & (col < end)
        rows = pl.ds(pl.multiple_of(t * TILE, TILE), TILE)
        span = pl.ds(pl.multiple_of(t * TILE, TILE), 2 * TILE)
        for pair in range(HEADS // 2):
            lanes = slice(pair * 128, (pair + 1) * 128)
            q = q_ref[rows, lanes]
            zero = jnp.zeros_like(q)
            stacked = jnp.concatenate([jnp.where(low_q, q, zero), jnp.where(low_q, zero, q)], 0)
            scores = jnp.where(allowed, mm_nt(stacked, k_ref[span, lanes]), masked_value)
            raised = jnp.exp(scores - jnp.max(scores, axis=-1, keepdims=True))
            probs = (raised / jnp.sum(raised, axis=-1, keepdims=True)).astype(BF16)
            prob_ref[t, pair] = probs
            v = v_ref[span, lanes]
            none = jnp.zeros_like(v)
            att_ref[rows, lanes] = mm(
                jnp.concatenate([probs[:TILE], probs[TILE:]], 1),
                jnp.concatenate([jnp.where(low_k, v, none), jnp.where(low_k, none, v)], 0),
            ).astype(BF16)
        return carry

    lax.fori_loop(0, ROWS // TILE, tile_step, 0)


def mlp_kernel(where_ref, att_ref, x_ref, gain_ref, cot_ref, att_own, in_own, out_own, first, second,
               hidden_out, up_out, send_out, keep_out, layer_out,
               w_att, w_in, w_out, normed, mixed, act_s, gate_s, dmix_s, sems):
    att_copies = place_weight(where_ref, (att_own, first, second), w_att, sems.at[0])
    in_copies = place_weight(where_ref, (in_own, first, second), w_in, sems.at[1], 240, 3)
    out_copies = place_weight(where_ref, (out_own, first, second), w_out, sems.at[2], 96)
    core = where_ref[1]
    hidden_ref, d_up, layer_ref = hidden_out.ref, up_out.ref, layer_out.ref
    att_ref, x_ref, gain = att_ref(), x_ref(), gain_ref()[...]
    for copy in att_copies:
        copy.wait()
    for j in range(3):
        cols = slice(j * 256, (j + 1) * 256)
        hidden_ref[:, cols] = x_ref[:, cols].astype(F32) + mm(att_ref[...], w_att[:, cols])
    hidden_out.send()

    def normalize(rows):
        normal, _ = ln_stats(hidden_ref[rows, :])
        normed[rows, :] = (normal * gain).astype(BF16)

    rows_loop(ROWS, 128, normalize)
    cot_ref = cot_ref()
    for copy in in_copies + out_copies:
        copy.wait()
    for j in range(3):
        cols = slice(j * 384, (j + 1) * 384)
        gates = slice(FF + j * 384, FF + (j + 1) * 384)
        act_s[...] = mm(normed[...], w_in[:, cols])
        gate_s[...] = mm(normed[...], w_in[:, gates])
        dmix_s[...] = mm_nt(cot_ref[...], w_out[cols, :])

        def gate(rows):
            act, gated_by, d_mixed = act_s[rows, :], gate_s[rows, :], dmix_s[rows, :]
            cumulative = 0.5 * (1.0 + lax.erf(act * 0.7071067811865476))
            density = jnp.exp(-0.5 * act * act) * 0.3989422804014327
            curved = act * cumulative
            mixed[rows, cols] = (curved * gated_by).astype(BF16)
            d_up[rows, cols] = (d_mixed * gated_by * (cumulative + act * density)).astype(BF16)
            d_up[rows, gates] = (d_mixed * curved).astype(BF16)

        rows_loop(ROWS, 128, gate)
    up_out.send()
    for out, which in ((send_out, 1 - core), (keep_out, core)):
        for j in range(3):
            cols = pl.ds(pl.multiple_of(which * 1152 + j * 384, 128), 384)
            grad = mm_tn(normed[...], d_up[:, cols]).astype(BF16)
            out.ref[:, :, j * 96 : (j + 1) * 96] = grad.reshape(2, 4, 96, 384)
        cols = pl.ds(pl.multiple_of(which * 384, 128), 384)
        grad = mm_tn(mixed[...], cot_ref[:, cols]).astype(BF16)
        out.ref[:, :, 288:] = grad.reshape(2, 4, 144, 384)
        out.send()
    for j in range(3):
        cols = slice(j * 256, (j + 1) * 256)
        layer_ref[:, cols] = (hidden_ref[:, cols] + mm(mixed[...], w_out[:, cols])).astype(BF16)


def mlp_back_kernel(where_ref, up_ref, hidden_ref, cot_ref, gain_ref, in_own, first, second,
                    dhid_out, w_in, dnorm_s, sems):
    copies = place_weight(where_ref, (in_own, first, second), w_in, sems, 240, 3)
    d_up = up_ref()
    for copy in copies:
        copy.wait()
    for j in range(3):
        cols = slice(j * 256, (j + 1) * 256)
        dnorm_s[:, cols] = mm_nt(d_up[...], w_in[cols, :])
    hidden_ref, cot_ref, gain = hidden_ref(), cot_ref(), gain_ref()[...]

    def back(rows):
        normal, scale = ln_stats(hidden_ref[rows, :])
        dhid_out.ref[rows, :] = cot_ref[rows, :].astype(F32) + ln_back(dnorm_s[rows, :], gain, normal, scale)

    rows_loop(ROWS, 128, back)


def attend_back_kernel(where_ref, dhid_ref, q_ref, k_ref, v_ref, prob_ref, cos_ref, sin_ref, att_ref, normed_ref,
                       own, first, second, dproj_out, edge_out, send_out, keep_out,
                       full, branch, datt, dkey, dvalue, grads_s, sems):
    copies = place_weight(where_ref, (own, first, second), full, sems)
    half, core = where_ref[0], where_ref[1]
    dproj_ref, edge_ref = dproj_out.ref, edge_out.ref
    dkey[...] = jnp.zeros_like(dkey)
    dvalue[...] = jnp.zeros_like(dvalue)
    for copy in copies:
        copy.wait()
    branch[...] = dhid_ref()[...].astype(BF16)
    for j in range(3):
        cols = slice(j * 256, (j + 1) * 256)
        datt[:, cols] = mm_nt(branch[...], full[cols, :]).astype(BF16)
    q_ref, k_ref, v_ref, prob_ref, cos_ref, sin_ref = (
        ref() for ref in (q_ref, k_ref, v_ref, prob_ref, cos_ref, sin_ref)
    )
    low_q, low_k = low_lanes(TILE, 128), low_lanes(2 * TILE, 128)
    turn_q = low_lanes(TILE, HEAD_DIM)

    def split(tile, low, axis=0):
        none = jnp.zeros_like(tile)
        return jnp.concatenate([jnp.where(low, tile, none), jnp.where(low, none, tile)], axis)

    def tile_step(t, carry):
        rows = pl.ds(pl.multiple_of(t * TILE, TILE), TILE)
        span = pl.ds(pl.multiple_of(t * TILE, TILE), 2 * TILE)
        cos, sin = cos_ref[rows, :], sin_ref[rows, :]
        for pair in range(HEADS // 2):
            lanes = slice(pair * 128, (pair + 1) * 128)
            grads = split(datt[rows, lanes], low_q)
            probs_b = prob_ref[t, pair]
            probs = probs_b.astype(F32)
            d_probs = mm_nt(grads, v_ref[span, lanes])
            delta = jnp.sum(probs * d_probs, axis=-1, keepdims=True)
            d_scores = (probs * (d_probs - delta)).astype(BF16)
            d_query = 0.125 * mm(
                jnp.concatenate([d_scores[:TILE], d_scores[TILE:]], 1), split(k_ref[span, lanes], low_k)
            )
            dproj_ref[rows, lanes] = (d_query * cos - turned(d_query, turn_q) * sin).astype(BF16)
            dkey[span, lanes] += mm_tn(d_scores, split(q_ref[rows, lanes], low_q))
            dvalue[span, lanes] += mm_tn(probs_b, grads)
        return carry

    lax.fori_loop(0, ROWS // TILE, tile_step, 0)
    turn_k = low_lanes(ROWS, HEAD_DIM)
    turn_e = low_lanes(HALF_WIN, HEAD_DIM)
    edge = pl.ds(pl.multiple_of((1 - half) * (ROWS + HALF_WIN), HALF_WIN), HALF_WIN)
    for pair in range(HEADS // 2):
        lanes = slice(pair * 128, (pair + 1) * 128)
        tile = dkey[HALF_WIN : HALF_WIN + ROWS, lanes]
        dproj_ref[:, 768 + pair * 128 : 768 + (pair + 1) * 128] = (
            tile * cos_ref[:ROWS] - turned(tile, turn_k) * sin_ref[:ROWS]
        ).astype(BF16)
        dproj_ref[:, 1536 + pair * 128 : 1536 + (pair + 1) * 128] = dvalue[
            HALF_WIN : HALF_WIN + ROWS, lanes
        ].astype(BF16)
        tile = dkey[edge, lanes]
        edge_ref[:, lanes] = (tile * cos_ref[ROWS:] - turned(tile, turn_e) * sin_ref[ROWS:]).astype(BF16)
        edge_ref[:, 768 + pair * 128 : 768 + (pair + 1) * 128] = dvalue[edge, lanes].astype(BF16)
    edge_out.send()
    dproj_out.send()
    normed_ref, att_ref = normed_ref(), att_ref()
    grads_s[:ROWS, :] = dproj_ref[...]
    grads_s[ROWS:, :768] = jnp.zeros((HALF_WIN, 768), BF16)
    grads_s[ROWS:, 768:] = edge_ref[...]
    for out, which in ((send_out, 1 - core), (keep_out, core)):
        for j in range(3):
            cols = pl.ds(pl.multiple_of(which * 1152 + j * 384, 128), 384)
            grad = mm_tn(normed_ref[...], grads_s[:, cols]).astype(BF16)
            out.ref[:, :, j * 96 : (j + 1) * 96] = grad.reshape(2, 4, 96, 384)
        cols = pl.ds(pl.multiple_of(which * 384, 128), 384)
        grad = mm_tn(att_ref[...], branch[:, cols]).astype(BF16)
        out.ref[:, :, 288:] = grad.reshape(2, 4, 96, 384)
        out.send()


def token_grad_kernel(where_ref, x_ref, gain_ref, dproj_ref, edge_ref, dhid_ref, own, first, second,
                      out, full, dnorm, sems):
    copies = place_weight(where_ref, (own, first, second), full, sems)
    grads, edge_ref = dproj_ref(), edge_ref()
    edge = pl.ds(pl.multiple_of((1 - where_ref[0]) * (ROWS - HALF_WIN), HALF_WIN), HALF_WIN)
    grads[edge, 768:] = (grads[edge, 768:].astype(F32) + edge_ref[...].astype(F32)).astype(BF16)
    for copy in copies:
        copy.wait()
    for j in range(3):
        cols = slice(j * 256, (j + 1) * 256)
        dnorm[:, cols] = mm_nt(grads[...], full[cols, :])

    gain, x_ref, dhid_ref = gain_ref()[...], x_ref(), dhid_ref()

    def back(rows):
        normal, scale = ln_stats(x_ref[rows, :].astype(F32))
        out.ref[rows, :] = (dhid_ref[rows, :] + ln_back(dnorm[rows, :], gain, normal, scale)).astype(BF16)

    rows_loop(ROWS, 128, back)


def finish_kernel(where_ref, mine, other, weight, gain, wide_out, narrow_out, gain_out):
    core = where_ref[1]
    wide_ref, narrow_ref = wide_out.ref, narrow_out.ref
    rows = narrow_ref.shape[0]
    for staged, which in ((mine, core), (other, 1 - core)):
        source = staged()
        for j in range(3):
            cols = pl.ds(pl.multiple_of(which * 1152 + j * 384, 128), 384)
            wide_ref[:, cols] = source[:, j * 96 : (j + 1) * 96].reshape(384, 384).astype(F32)
        cols = pl.ds(pl.multiple_of(which * 384, 128), 384)
        narrow_ref[:, cols] = source[:, 288:].reshape(rows, 384).astype(F32)
    wide_out.send()
    narrow_out.send()
    gain_rows(wide_ref, weight(), gain(), gain_out.ref)


def gain_rows(grad_ref, weight, gain, gain_ref):
    for n in range(3):
        rows = slice(n * 128, (n + 1) * 128)
        total = jnp.sum(grad_ref[rows, :] * weight[rows, :].astype(F32), axis=-1, keepdims=True)
        gain_ref[rows] = (jnp.broadcast_to(total, (128, 128)).T[:1] / gain[:, rows].astype(F32))[0]


class Staged:
    def __init__(self, source, ref, sem):
        self.ref, self.copy, self.there = ref, pltpu.make_async_copy(source, ref, sem), False
        self.copy.start()

    def __call__(self):
        if not self.there:
            self.copy.wait()
            self.there = True
        return self.ref


class Result:
    def __init__(self, ref, target, sem):
        self.ref, self.copy, self.sent = ref, pltpu.make_async_copy(ref, target, sem), False

    def send(self):
        if not self.sent:
            self.copy.start()
            self.sent = True


def run(kernel, ins, outs, scratch, flops):
    staged = [a for a, kind in ins if kind == "v"]
    spaces = {"s": pltpu.SMEM, "h": pl.ANY, "v": pl.ANY}
    moved = sum(a.size * a.dtype.itemsize for a, _ in ins) + sum(
        math.prod(shape) * jnp.dtype(dtype).itemsize for shape, dtype in outs
    )

    def body(*refs):
        given, refs = refs[: len(ins)], refs[len(ins) :]
        targets, refs = refs[: len(outs)], refs[len(outs) :]
        places, refs = refs[: len(staged)], refs[len(staged) :]
        ready, refs = refs[: len(outs)], refs[len(outs) :]
        in_sems, out_sems, *rest = refs
        taken, n = [], 0
        for ref, (_, kind) in zip(given, ins):
            if kind == "v":
                ref = Staged(ref, places[n], in_sems.at[n])
                n += 1
            taken.append(ref)
        results = [Result(r, t, out_sems.at[k]) for k, (r, t) in enumerate(zip(ready, targets))]
        kernel(*taken, *results, *rest)
        for ref in taken:
            if isinstance(ref, Staged):
                ref()
        for result in results:
            result.send()
        for result in results:
            result.copy.wait()

    dma = pltpu.SemaphoreType.DMA
    return pl.pallas_call(
        body,
        in_specs=[pl.BlockSpec(memory_space=spaces[kind]) for _, kind in ins],
        out_specs=[pl.BlockSpec(memory_space=pl.ANY) for _ in outs],
        out_shape=[jax.ShapeDtypeStruct(shape, dtype) for shape, dtype in outs],
        scratch_shapes=[pltpu.VMEM(a.shape, a.dtype) for a in staged]
        + [pltpu.VMEM(shape, dtype) for shape, dtype in outs]
        + [dma((len(staged),)), dma((len(outs),))]
        + scratch,
        compiler_params=pltpu.CompilerParams(vmem_limit_bytes=60 * 1024 * 1024),
        cost_estimate=pl.CostEstimate(flops=int(flops), bytes_accessed=int(moved), transcendentals=0),
    )(*[a for a, _ in ins])


def together(*arrays):
    return lax.optimization_barrier(arrays)


def block_of(own):
    rows, cols = own.shape
    index = lax.axis_index(CORE) * 2 + (lax.axis_index(XAXIS) & 1)
    return pick(own.reshape(4, rows // 4, cols), index, 0)


def beside_x(block, come):
    return ordered(block, come, lax.axis_index(XAXIS) & 1, 0)


def total_rows(send, keep, shape, first_axis, last_axis):
    core, half = lax.axis_index(CORE), lax.axis_index(FAR)
    near, place = lax.axis_index(NEAR) ^ half, lax.axis_index(first_axis)
    first_bit = jnp.where(core == 0, ((place + 1) >> 1) & 1, place >> 1)
    second_bit = place & 1
    send = yield send
    keep, come = keep.reshape(shape), core_swap(send).reshape(shape)
    for bit, first in ((first_bit, True), (second_bit, False)):
        send = yield add(pick(keep, 1 - bit, 1), pick(come, 1 - bit, 1))
        keep, come = add(pick(keep, bit, 1), pick(come, bit, 1)), ring_swap(send, first_axis, first)
    keep, come = (a.reshape((4,) + shape[4:]) for a in (keep, come))

    def two(which_half, which_near):
        index = [jnp.where(core == 0, which_half * 2 + i, i * 2 + which_near) for i in range(2)]
        return jnp.stack([add(pick(keep, i, 0), pick(come, i, 0)) for i in index])

    send = yield two(1 - half, 1 - near)
    keep, come = two(half, near), depth_swap(send, True)
    bit = jnp.where(core == 0, near, half)
    send = yield add(pick(keep, 1 - bit, 0), pick(come, 1 - bit, 0))
    keep, come = add(pick(keep, bit, 0), pick(come, bit, 0)), depth_swap(send, False)
    for first in (True, False):
        send = yield add(keep, come)
        keep, come = send, ring_swap(send, last_axis, first)
    send = yield add(keep, come)
    send = yield ordered(send, lax.ppermute(send, NEAR, SWAP), near, 0)
    send = yield ordered(send, ring_swap(send, first_axis, False), second_bit, 0)
    come = yield ring_swap(send, first_axis, True)
    send = yield ordered(send, come, first_bit, 0)
    yield send, core_swap(send)


def local(tokens, norm_gain_one, qkv_weight, attn_out_weight, norm_gain_two, in_weight, mlp_out_weight, cotangent):
    core, half = lax.axis_index(CORE), lax.axis_index(FAR)
    where = jnp.stack([half, core]).astype(jnp.int32)
    block = across_halves(block_of(qkv_weight))
    in_own = block_of(in_weight)
    rest_own = jnp.concatenate(
        [block_of(attn_out_weight), block_of(mlp_out_weight)] + [in_own[:, n * 768 : (n + 1) * 768] for n in range(3)], 0
    )
    edge = jnp.where(half == 0, tokens[ROWS - HALF_WIN :], tokens[:HALF_WIN])
    gains = jnp.pad(jnp.stack([norm_gain_one, norm_gain_two]), ((0, 14), (0, 384)))
    edge, rest_own = together(jnp.concatenate([edge, gains], 0), rest_own)
    beside = lax.ppermute(edge, FAR, SWAP)
    block, rest_own, beside = together(block, rest_own, beside)
    rest = across_halves(rest_own)
    both = beside_x(block, ring_swap(block, XAXIS, True))
    qkv = (qkv_weight, both, core_swap(both))
    fetched = beside[HALF_WIN:, :384]
    beside = beside[:HALF_WIN]
    gain_one = ordered(norm_gain_one, fetched[0], half, 0).reshape(1, 768).astype(F32)
    gain_two = ordered(norm_gain_two, fetched[1], half, 0).reshape(1, 768).astype(F32)
    index = jnp.arange(ROWS + HALF_WIN, dtype=jnp.int32)
    position = jnp.where(index < ROWS, half * ROWS + index, jnp.where(half == 0, index, index - HALF_WIN))
    lane = jnp.arange(128, dtype=jnp.int32)
    frequency = theta ** (-((lane % 32).astype(F32) * 2.0 / HEAD_DIM))
    angles = position.astype(F32)[:, None] * frequency[None, :]
    cosine = jnp.cos(angles)
    sine = jnp.where((lane % HEAD_DIM) < HEAD_DIM // 2, -1.0, 1.0) * jnp.sin(angles)

    h = lambda arrays: [(a, "h") for a in arrays]
    v = lambda *arrays: [(a, "v") for a in arrays]
    s = [(where, "s")]
    dma = pltpu.SemaphoreType.DMA
    wide, narrow, tall = pltpu.VMEM((768, 2304), BF16), pltpu.VMEM((768, 768), BF16), pltpu.VMEM((1152, 768), BF16)
    normed, query, key, value = run(
        qkv_kernel, s + v(tokens, beside, gain_one, cosine, sine) + h(qkv),
        [((ROWS + HALF_WIN, 768), BF16), ((ROWS, 768), BF16), ((640, 768), BF16), ((640, 768), BF16)],
        [wide, dma((5,))], 2 * 576 * 768 * 2304,
    )
    query, rest = together(query, rest)
    attended, probs = run(
        attend_kernel, s + v(query, key, value),
        [((ROWS, 768), BF16), ((4, 6, 256, 256), BF16)], [], 2 * 512 * 768 * 1024,
    )
    attended, come = together(attended, ring_swap(rest, XAXIS, True))
    both = beside_x(rest, come)
    rest = [both, core_swap(both)]
    hidden, d_up, send, keep, layer_output = run(
        mlp_kernel,
        s + v(attended, tokens, gain_two, cotangent) + h([attn_out_weight, in_weight, mlp_out_weight] + rest),
        [((ROWS, 768), F32), ((ROWS, 2 * FF), BF16), ((2, 4, 432, 384), BF16), ((2, 4, 432, 384), BF16),
         ((ROWS, 768), BF16)],
        [narrow, wide, tall, pltpu.VMEM((ROWS, 768), BF16), pltpu.VMEM((ROWS, FF), BF16),
         pltpu.VMEM((ROWS, 384), F32), pltpu.VMEM((ROWS, 384), F32), pltpu.VMEM((ROWS, 384), F32), dma((3, 13))],
        2 * 512 * 768 * 6600,
    )
    early = total_rows(send, keep, (2, 2, 2, 2, 216, 384), YAXIS, XAXIS)
    early_next = early.send(early.send(None))
    (d_hidden,) = run(
        mlp_back_kernel, s + v(d_up, hidden, cotangent, gain_two) + h([in_weight] + rest),
        [((ROWS, 768), F32)], [wide, pltpu.VMEM((ROWS, 768), F32), dma((13,))], 2 * 512 * 768 * 2304,
    )
    early_sent, d_hidden = together(early_next, d_hidden)
    early_next = early.send(early_sent)
    d_projected, edge_grad, send, keep = run(
        attend_back_kernel,
        s + v(d_hidden, query, key, value, probs, cosine, sine, attended, normed) + h([attn_out_weight] + rest),
        [((ROWS, 2304), BF16), ((HALF_WIN, 1536), BF16), ((2, 4, 384, 384), BF16), ((2, 4, 384, 384), BF16)],
        [narrow, pltpu.VMEM((ROWS, 768), BF16), pltpu.VMEM((ROWS, 768), BF16), pltpu.VMEM((640, 768), F32),
         pltpu.VMEM((640, 768), F32), pltpu.VMEM((ROWS + HALF_WIN, 2304), BF16), dma((5,))],
        2 * 512 * 768 * (768 + 2048 + 2304 + 768),
    )
    late = total_rows(send, keep, (2, 2, 2, 2, 192, 384), XAXIS, YAXIS)
    late_sent, early_sent = together(late.send(None), early_next)
    edge_grad = lax.ppermute(edge_grad, FAR, SWAP)
    late_sent, early_sent = late.send(late_sent), early.send(early_sent)
    (token_grad,) = run(
        token_grad_kernel, s + v(tokens, gain_one, d_projected, edge_grad, d_hidden) + h(qkv),
        [((ROWS, 768), BF16)],
        [wide, pltpu.VMEM((ROWS, 768), F32), dma((5,))], 2 * 512 * 768 * 2304,
    )
    late_next, early_next = late.send(late_sent), early.send(early_sent)
    late_next, early_next, token_grad = together(late_next, early_next, token_grad)
    while not isinstance(early_next, tuple):
        early_next = early.send(early_next)

    def finish(pair, weight, gain, rows):
        return run(
            finish_kernel,
            s + v(*(a.reshape(4, -1, 384) for a in pair), weight, gain.reshape(1, 384)),
            [((384, 2304), F32), ((rows, 768), F32), ((384,), F32)], [], 0,
        )

    in_sum, mlp_out_sum, gain_two_sum = finish(early_next, in_weight, norm_gain_two, 576)
    for _ in range(8):
        late_next = late.send(late_next)
    late_next, in_sum = together(late_next, in_sum)
    for _ in range(2):
        late_next = late.send(late_next)
    qkv_sum, attn_out_sum, gain_one_sum = finish(late_next, qkv_weight, norm_gain_one, 384)
    return (
        layer_output,
        token_grad,
        gain_one_sum,
        qkv_sum,
        attn_out_sum,
        gain_two_sum,
        in_sum,
        mlp_out_sum,
    )


def solution(mesh):
    fine = jax.sharding.Mesh(
        mesh.devices.reshape(4, 4, 2, 2, 2), (YAXIS, XAXIS, NEAR, CORE, FAR)
    )
    every = P((YAXIS, XAXIS, NEAR, CORE, FAR), None)
    return jax.shard_map(
        local,
        mesh=fine,
        in_specs=(every, P(FAR), P(FAR, None), P(FAR, None), P(FAR), P(FAR, None), P(FAR, None), every),
        out_specs=(every, every, P(FAR), P(FAR, None), P(FAR, None), P(FAR), P(FAR, None), P(FAR, None)),
        check_vma=False,
    )
```

```python
import math

import jax
import jax.numpy as jnp
from jax import lax
from jax.experimental import pallas as pl
from jax.experimental.pallas import tpu as pltpu
from jax.sharding import PartitionSpec as P

HEADS = 12
HEAD_DIM = 64
FF = 1152
HALF_WIN = 64
TILE = 2 * HALF_WIN
ROWS = 512
F32, BF16 = jnp.float32, jnp.bfloat16

eps_norm = 1e-05
theta = 10000.0
masked_value = -1e30

YAXIS, XAXIS, NEAR, CORE, FAR = "y", "x", "zl", "c", "zh"
PAIRS_A = [(0, 1), (1, 0), (2, 3), (3, 2)]
PAIRS_B = [(0, 3), (3, 0), (1, 2), (2, 1)]
SWAP = [(0, 1), (1, 0)]


def ring_swap(x, axis, first):
    even, odd = (PAIRS_A, PAIRS_B) if first else (PAIRS_B, PAIRS_A)
    if axis == YAXIS:
        pairs = [
            ((i * 4 + k) * 4 + r, (j * 4 + k) * 4 + r)
            for z in range(2)
            for c, group in ((0, even), (1, odd))
            for r in (z * 2 + c,)
            for k in range(4)
            for i, j in group
        ]
        return lax.ppermute(x, (YAXIS, XAXIS, NEAR, CORE), pairs)
    pairs = [
        (i * 4 + z * 2 + c, j * 4 + z * 2 + c)
        for z in range(2)
        for c, group in ((0, even), (1, odd))
        for i, j in group
    ]
    return lax.ppermute(x, (XAXIS, NEAR, CORE), pairs)


def depth_swap(x, first):
    across = [(i, 3 - i) for i in range(4)]
    within = [(i, i ^ 2) for i in range(4)]
    even, odd = (across, within) if first else (within, across)
    pairs = []
    for c, group in ((0, even), (1, odd)):
        for i, j in group:
            pairs.append(((i >> 1) * 4 + c * 2 + (i & 1), (j >> 1) * 4 + c * 2 + (j & 1)))
    return lax.ppermute(x, (NEAR, CORE, FAR), pairs)


def across_halves(x):
    return lax.ppermute(x, (NEAR, FAR), [(i, 3 - i) for i in range(4)])


def core_swap(x):
    return lax.ppermute(x, CORE, SWAP)


def pick(x, index, axis):
    return lax.dynamic_index_in_dim(x, index, axis, keepdims=False)


def ordered(mine, other, index, axis):
    return jnp.where(index == 0, jnp.stack([mine, other], axis), jnp.stack([other, mine], axis))


def add(a, b):
    return (a.astype(jnp.float32) + b.astype(jnp.float32)).astype(jnp.bfloat16)


def ln_stats(v):
    mean = jnp.mean(v, axis=-1, keepdims=True)
    centred = v - mean
    scale = lax.rsqrt(jnp.mean(centred * centred, axis=-1, keepdims=True) + eps_norm)
    return centred * scale, scale


def ln_back(grad, gain, normal, scale):
    inner = grad * gain
    mean_inner = jnp.mean(inner, axis=-1, keepdims=True)
    mean_cross = jnp.mean(inner * normal, axis=-1, keepdims=True)
    return scale * (inner - mean_inner - normal * mean_cross)


def mm(a, b):
    return jnp.dot(a, b, preferred_element_type=F32)


def mm_nt(a, b):
    return lax.dot_general(a, b, (((1,), (1,)), ((), ())), preferred_element_type=F32)


def mm_tn(a, b):
    return lax.dot_general(a, b, (((0,), (0,)), ((), ())), preferred_element_type=F32)


def rows_loop(rows, chunk, body):
    def step(i, carry):
        body(pl.ds(pl.multiple_of(i * chunk, chunk), chunk))
        return carry

    lax.fori_loop(0, rows // chunk, step, 0)


def place_weight(where_ref, pieces, full, sems, skip=0, parts=1):
    half, core = where_ref[0], where_ref[1]
    own, mine, others = pieces
    rows, cols = own.shape[0], own.shape[1] // parts
    block = rows // 4
    other = (1 - half) * rows
    copies = [pltpu.make_async_copy(own, full.at[pl.ds(pl.multiple_of(half * rows, 16), rows)], sems.at[0])]
    for source, which in ((mine, core), (others, 1 - core)):
        for b in range(2):
            place = pl.ds(pl.multiple_of(other + (which * 2 + b) * block, 16), block)
            for j in range(parts):
                copies.append(
                    pltpu.make_async_copy(
                        source.at[b, pl.ds(skip + j * block, block)],
                        full.at[place, pl.ds(j * cols, cols)],
                        sems.at[len(copies)],
                    )
                )
    for copy in copies:
        copy.start()
    return copies


def turned(tile, lane):
    return jnp.where(lane, pltpu.roll(tile, 96, 1), pltpu.roll(tile, 32, 1))


def low_lanes(rows, period):
    lanes = lax.broadcasted_iota(jnp.int32, (rows, 128), 1)
    return (lanes % period) < period // 2


def qkv_kernel(where_ref, x_ref, beside_ref, gain_ref, cos_ref, sin_ref, own, first, second,
               normed_out, query_out, key_out, value_out, full, sems):
    copies = place_weight(where_ref, (own, first, second), full, sems)
    normed, query_ref, key_ref, value_ref = (out.ref for out in (normed_out, query_out, key_out, value_out))
    gain, x_ref, beside_ref = gain_ref()[...], x_ref(), beside_ref()

    def main(rows):
        normal, _ = ln_stats(x_ref[rows, :].astype(F32))
        normed[rows, :] = (normal * gain).astype(BF16)

    rows_loop(ROWS, 128, main)
    normal, _ = ln_stats(beside_ref[...].astype(F32))
    normed[ROWS:, :] = (normal * gain).astype(BF16)
    normed_out.send()
    for copy in copies:
        copy.wait()
    cos_ref, sin_ref = cos_ref(), sin_ref()
    lane = low_lanes(ROWS + HALF_WIN, HEAD_DIM)
    for j in range(9):
        cols = slice(j * 256, (j + 1) * 256)
        proj = mm(normed[...], full[:, cols])
        for side in range(2):
            tile = proj[:, side * 128 : (side + 1) * 128]
            if j < 6:
                tile = tile * cos_ref[...] + turned(tile, lane) * sin_ref[...]
            place = slice((j % 3) * 256 + side * 128, (j % 3) * 256 + (side + 1) * 128)
            if j < 3:
                query_ref[:, place] = (tile[:ROWS] * 0.125).astype(BF16)
            else:
                out_ref = key_ref if j < 6 else value_ref
                edge = tile[ROWS:].astype(BF16)
                out_ref[HALF_WIN : HALF_WIN + ROWS, place] = tile[:ROWS].astype(BF16)
                out_ref[:HALF_WIN, place] = edge
                out_ref[HALF_WIN + ROWS :, place] = edge
        if j == 2:
            query_out.send()
        if j == 5:
            key_out.send()


def attend_kernel(where_ref, q_ref, k_ref, v_ref, att_out, prob_out):
    att_ref, prob_ref = att_out.ref, prob_out.ref
    q_ref, k_ref, v_ref = q_ref(), k_ref(), v_ref()
    half = where_ref[0]
    low_q, low_k = low_lanes(TILE, 128), low_lanes(2 * TILE, 128)
    row = lax.broadcasted_iota(jnp.int32, (2 * TILE, 2 * TILE), 0) % TILE
    col = lax.broadcasted_iota(jnp.int32, (2 * TILE, 2 * TILE), 1)
    band = (col >= row) & (col <= row + 2 * HALF_WIN)

    def tile_step(t, carry):
        begin = jnp.where((half == 0) & (t == 0), HALF_WIN, 0)
        end = jnp.where((half == 1) & (t == ROWS // TILE - 1), 2 * TILE - HALF_WIN, 2 * TILE)
        allowed = band & (col >= begin) & (col < end)
        rows = pl.ds(pl.multiple_of(t * TILE, TILE), TILE)
        span = pl.ds(pl.multiple_of(t * TILE, TILE), 2 * TILE)
        for pair in range(HEADS // 2):
            lanes = slice(pair * 128, (pair + 1) * 128)
            q = q_ref[rows, lanes]
            zero = jnp.zeros_like(q)
            stacked = jnp.concatenate([jnp.where(low_q, q, zero), jnp.where(low_q, zero, q)], 0)
            scores = jnp.where(allowed, mm_nt(stacked, k_ref[span, lanes]), masked_value)
            raised = jnp.exp(scores - jnp.max(scores, axis=-1, keepdims=True))
            probs = (raised / jnp.sum(raised, axis=-1, keepdims=True)).astype(BF16)
            prob_ref[t, pair] = probs
            v = v_ref[span, lanes]
            none = jnp.zeros_like(v)
            att_ref[rows, lanes] = mm(
                jnp.concatenate([probs[:TILE], probs[TILE:]], 1),
                jnp.concatenate([jnp.where(low_k, v, none), jnp.where(low_k, none, v)], 0),
            ).astype(BF16)
        return carry

    lax.fori_loop(0, ROWS // TILE, tile_step, 0)


def mlp_kernel(where_ref, att_ref, x_ref, gain_ref, cot_ref, att_own, in_own, out_own, first, second,
               hidden_out, up_out, send_out, keep_out, layer_out,
               w_att, w_in, w_out, normed, mixed, act_s, gate_s, dmix_s, sems):
    att_copies = place_weight(where_ref, (att_own, first, second), w_att, sems.at[0])
    in_copies = place_weight(where_ref, (in_own, first, second), w_in, sems.at[1], 240, 3)
    out_copies = place_weight(where_ref, (out_own, first, second), w_out, sems.at[2], 96)
    core = where_ref[1]
    hidden_ref, d_up, layer_ref = hidden_out.ref, up_out.ref, layer_out.ref
    att_ref, x_ref, gain = att_ref(), x_ref(), gain_ref()[...]
    for copy in att_copies:
        copy.wait()
    for j in range(3):
        cols = slice(j * 256, (j + 1) * 256)
        hidden_ref[:, cols] = x_ref[:, cols].astype(F32) + mm(att_ref[...], w_att[:, cols])
    hidden_out.send()

    def normalize(rows):
        normal, _ = ln_stats(hidden_ref[rows, :])
        normed[rows, :] = (normal * gain).astype(BF16)

    rows_loop(ROWS, 128, normalize)
    cot_ref = cot_ref()
    for copy in in_copies + out_copies:
        copy.wait()
    for j in range(3):
        cols = slice(j * 384, (j + 1) * 384)
        gates = slice(FF + j * 384, FF + (j + 1) * 384)
        act_s[...] = mm(normed[...], w_in[:, cols])
        gate_s[...] = mm(normed[...], w_in[:, gates])
        dmix_s[...] = mm_nt(cot_ref[...], w_out[cols, :])

        def gate(rows):
            act, gated_by, d_mixed = act_s[rows, :], gate_s[rows, :], dmix_s[rows, :]
            cumulative = 0.5 * (1.0 + lax.erf(act * 0.7071067811865476))
            density = jnp.exp(-0.5 * act * act) * 0.3989422804014327
            curved = act * cumulative
            mixed[rows, cols] = (curved * gated_by).astype(BF16)
            d_up[rows, cols] = (d_mixed * gated_by * (cumulative + act * density)).astype(BF16)
            d_up[rows, gates] = (d_mixed * curved).astype(BF16)

        rows_loop(ROWS, 128, gate)
    up_out.send()
    for out, which in ((send_out, 1 - core), (keep_out, core)):
        for j in range(3):
            cols = pl.ds(pl.multiple_of(which * 1152 + j * 384, 128), 384)
            grad = mm_tn(normed[...], d_up[:, cols]).astype(BF16)
            out.ref[:, :, j * 96 : (j + 1) * 96] = grad.reshape(2, 4, 96, 384)
        cols = pl.ds(pl.multiple_of(which * 384, 128), 384)
        grad = mm_tn(mixed[...], cot_ref[:, cols]).astype(BF16)
        out.ref[:, :, 288:] = grad.reshape(2, 4, 144, 384)
        out.send()
    for j in range(3):
        cols = slice(j * 256, (j + 1) * 256)
        layer_ref[:, cols] = (hidden_ref[:, cols] + mm(mixed[...], w_out[:, cols])).astype(BF16)


def mlp_back_kernel(where_ref, up_ref, hidden_ref, cot_ref, gain_ref, in_own, first, second,
                    dhid_out, w_in, dnorm_s, sems):
    copies = place_weight(where_ref, (in_own, first, second), w_in, sems, 240, 3)
    d_up = up_ref()
    for copy in copies:
        copy.wait()
    for j in range(3):
        cols = slice(j * 256, (j + 1) * 256)
        dnorm_s[:, cols] = mm_nt(d_up[...], w_in[cols, :])
    hidden_ref, cot_ref, gain = hidden_ref(), cot_ref(), gain_ref()[...]

    def back(rows):
        normal, scale = ln_stats(hidden_ref[rows, :])
        dhid_out.ref[rows, :] = cot_ref[rows, :].astype(F32) + ln_back(dnorm_s[rows, :], gain, normal, scale)

    rows_loop(ROWS, 128, back)


def attend_back_kernel(where_ref, dhid_ref, q_ref, k_ref, v_ref, prob_ref, cos_ref, sin_ref, att_ref, normed_ref,
                       own, first, second, dproj_out, edge_out, send_out, keep_out,
                       full, branch, datt, dkey, dvalue, grads_s, sems):
    copies = place_weight(where_ref, (own, first, second), full, sems)
    half, core = where_ref[0], where_ref[1]
    dproj_ref, edge_ref = dproj_out.ref, edge_out.ref
    dkey[...] = jnp.zeros_like(dkey)
    dvalue[...] = jnp.zeros_like(dvalue)
    for copy in copies:
        copy.wait()
    branch[...] = dhid_ref()[...].astype(BF16)
    for j in range(3):
        cols = slice(j * 256, (j + 1) * 256)
        datt[:, cols] = mm_nt(branch[...], full[cols, :]).astype(BF16)
    q_ref, k_ref, v_ref, prob_ref, cos_ref, sin_ref = (
        ref() for ref in (q_ref, k_ref, v_ref, prob_ref, cos_ref, sin_ref)
    )
    low_q, low_k = low_lanes(TILE, 128), low_lanes(2 * TILE, 128)
    turn_q = low_lanes(TILE, HEAD_DIM)

    def split(tile, low, axis=0):
        none = jnp.zeros_like(tile)
        return jnp.concatenate([jnp.where(low, tile, none), jnp.where(low, none, tile)], axis)

    def tile_step(t, carry):
        rows = pl.ds(pl.multiple_of(t * TILE, TILE), TILE)
        span = pl.ds(pl.multiple_of(t * TILE, TILE), 2 * TILE)
        cos, sin = cos_ref[rows, :], sin_ref[rows, :]
        for pair in range(HEADS // 2):
            lanes = slice(pair * 128, (pair + 1) * 128)
            grads = split(datt[rows, lanes], low_q)
            probs_b = prob_ref[t, pair]
            probs = probs_b.astype(F32)
            d_probs = mm_nt(grads, v_ref[span, lanes])
            delta = jnp.sum(probs * d_probs, axis=-1, keepdims=True)
            d_scores = (probs * (d_probs - delta)).astype(BF16)
            d_query = 0.125 * mm(
                jnp.concatenate([d_scores[:TILE], d_scores[TILE:]], 1), split(k_ref[span, lanes], low_k)
            )
            dproj_ref[rows, lanes] = (d_query * cos - turned(d_query, turn_q) * sin).astype(BF16)
            dkey[span, lanes] += mm_tn(d_scores, split(q_ref[rows, lanes], low_q))
            dvalue[span, lanes] += mm_tn(probs_b, grads)
        return carry

    lax.fori_loop(0, ROWS // TILE, tile_step, 0)
    turn_k = low_lanes(ROWS, HEAD_DIM)
    turn_e = low_lanes(HALF_WIN, HEAD_DIM)
    edge = pl.ds(pl.multiple_of((1 - half) * (ROWS + HALF_WIN), HALF_WIN), HALF_WIN)
    for pair in range(HEADS // 2):
        lanes = slice(pair * 128, (pair + 1) * 128)
        tile = dkey[HALF_WIN : HALF_WIN + ROWS, lanes]
        dproj_ref[:, 768 + pair * 128 : 768 + (pair + 1) * 128] = (
            tile * cos_ref[:ROWS] - turned(tile, turn_k) * sin_ref[:ROWS]
        ).astype(BF16)
        dproj_ref[:, 1536 + pair * 128 : 1536 + (pair + 1) * 128] = dvalue[
            HALF_WIN : HALF_WIN + ROWS, lanes
        ].astype(BF16)
        tile = dkey[edge, lanes]
        edge_ref[:, lanes] = (tile * cos_ref[ROWS:] - turned(tile, turn_e) * sin_ref[ROWS:]).astype(BF16)
        edge_ref[:, 768 + pair * 128 : 768 + (pair + 1) * 128] = dvalue[edge, lanes].astype(BF16)
    edge_out.send()
    dproj_out.send()
    normed_ref, att_ref = normed_ref(), att_ref()
    grads_s[:ROWS, :] = dproj_ref[...]
    grads_s[ROWS:, :768] = jnp.zeros((HALF_WIN, 768), BF16)
    grads_s[ROWS:, 768:] = edge_ref[...]
    for out, which in ((send_out, 1 - core), (keep_out, core)):
        for j in range(3):
            cols = pl.ds(pl.multiple_of(which * 1152 + j * 384, 128), 384)
            grad = mm_tn(normed_ref[...], grads_s[:, cols]).astype(BF16)
            out.ref[:, :, j * 96 : (j + 1) * 96] = grad.reshape(2, 4, 96, 384)
        cols = pl.ds(pl.multiple_of(which * 384, 128), 384)
        grad = mm_tn(att_ref[...], branch[:, cols]).astype(BF16)
        out.ref[:, :, 288:] = grad.reshape(2, 4, 96, 384)
        out.send()


def token_grad_kernel(where_ref, x_ref, gain_ref, dproj_ref, edge_ref, dhid_ref, own, first, second,
                      out, full, dnorm, sems):
    copies = place_weight(where_ref, (own, first, second), full, sems)
    grads, edge_ref = dproj_ref(), edge_ref()
    edge = pl.ds(pl.multiple_of((1 - where_ref[0]) * (ROWS - HALF_WIN), HALF_WIN), HALF_WIN)
    grads[edge, 768:] = (grads[edge, 768:].astype(F32) + edge_ref[...].astype(F32)).astype(BF16)
    for copy in copies:
        copy.wait()
    for j in range(3):
        cols = slice(j * 256, (j + 1) * 256)
        dnorm[:, cols] = mm_nt(grads[...], full[cols, :])

    gain, x_ref, dhid_ref = gain_ref()[...], x_ref(), dhid_ref()

    def back(rows):
        normal, scale = ln_stats(x_ref[rows, :].astype(F32))
        out.ref[rows, :] = (dhid_ref[rows, :] + ln_back(dnorm[rows, :], gain, normal, scale)).astype(BF16)

    rows_loop(ROWS, 128, back)


def finish_kernel(where_ref, mine, other, weight, gain, wide_out, narrow_out, gain_out):
    core = where_ref[1]
    wide_ref, narrow_ref = wide_out.ref, narrow_out.ref
    rows = narrow_ref.shape[0]
    for staged, which in ((mine, core), (other, 1 - core)):
        source = staged()
        for j in range(3):
            cols = pl.ds(pl.multiple_of(which * 1152 + j * 384, 128), 384)
            wide_ref[:, cols] = source[:, j * 96 : (j + 1) * 96].reshape(384, 384).astype(F32)
        cols = pl.ds(pl.multiple_of(which * 384, 128), 384)
        narrow_ref[:, cols] = source[:, 288:].reshape(rows, 384).astype(F32)
    wide_out.send()
    narrow_out.send()
    gain_rows(wide_ref, weight(), gain(), gain_out.ref)


def gain_rows(grad_ref, weight, gain, gain_ref):
    for n in range(3):
        rows = slice(n * 128, (n + 1) * 128)
        total = jnp.sum(grad_ref[rows, :] * weight[rows, :].astype(F32), axis=-1, keepdims=True)
        gain_ref[rows] = (jnp.broadcast_to(total, (128, 128)).T[:1] / gain[:, rows].astype(F32))[0]


class Staged:
    def __init__(self, source, ref, sem):
        self.ref, self.copy, self.there = ref, pltpu.make_async_copy(source, ref, sem), False
        self.copy.start()

    def __call__(self):
        if not self.there:
            self.copy.wait()
            self.there = True
        return self.ref


class Result:
    def __init__(self, ref, target, sem):
        self.ref, self.copy, self.sent = ref, pltpu.make_async_copy(ref, target, sem), False

    def send(self):
        if not self.sent:
            self.copy.start()
            self.sent = True


def run(kernel, ins, outs, scratch, flops):
    staged = [a for a, kind in ins if kind == "v"]
    spaces = {"s": pltpu.SMEM, "h": pl.ANY, "v": pl.ANY}
    moved = sum(a.size * a.dtype.itemsize for a, _ in ins) + sum(
        math.prod(shape) * jnp.dtype(dtype).itemsize for shape, dtype in outs
    )

    def body(*refs):
        given, refs = refs[: len(ins)], refs[len(ins) :]
        targets, refs = refs[: len(outs)], refs[len(outs) :]
        places, refs = refs[: len(staged)], refs[len(staged) :]
        ready, refs = refs[: len(outs)], refs[len(outs) :]
        in_sems, out_sems, *rest = refs
        taken, n = [], 0
        for ref, (_, kind) in zip(given, ins):
            if kind == "v":
                ref = Staged(ref, places[n], in_sems.at[n])
                n += 1
            taken.append(ref)
        results = [Result(r, t, out_sems.at[k]) for k, (r, t) in enumerate(zip(ready, targets))]
        kernel(*taken, *results, *rest)
        for ref in taken:
            if isinstance(ref, Staged):
                ref()
        for result in results:
            result.send()
        for result in results:
            result.copy.wait()

    dma = pltpu.SemaphoreType.DMA
    return pl.pallas_call(
        body,
        in_specs=[pl.BlockSpec(memory_space=spaces[kind]) for _, kind in ins],
        out_specs=[pl.BlockSpec(memory_space=pl.ANY) for _ in outs],
        out_shape=[jax.ShapeDtypeStruct(shape, dtype) for shape, dtype in outs],
        scratch_shapes=[pltpu.VMEM(a.shape, a.dtype) for a in staged]
        + [pltpu.VMEM(shape, dtype) for shape, dtype in outs]
        + [dma((len(staged),)), dma((len(outs),))]
        + scratch,
        compiler_params=pltpu.CompilerParams(vmem_limit_bytes=60 * 1024 * 1024),
        cost_estimate=pl.CostEstimate(flops=int(flops), bytes_accessed=int(moved), transcendentals=0),
    )(*[a for a, _ in ins])


def together(*arrays):
    return lax.optimization_barrier(arrays)


def block_of(own):
    rows, cols = own.shape
    index = lax.axis_index(CORE) * 2 + (lax.axis_index(XAXIS) & 1)
    return pick(own.reshape(4, rows // 4, cols), index, 0)


def beside_x(block, come):
    return ordered(block, come, lax.axis_index(XAXIS) & 1, 0)


def total_rows(send, keep, shape, first_axis, last_axis):
    core, half = lax.axis_index(CORE), lax.axis_index(FAR)
    near, place = lax.axis_index(NEAR) ^ half, lax.axis_index(first_axis)
    first_bit = jnp.where(core == 0, ((place + 1) >> 1) & 1, place >> 1)
    second_bit = place & 1
    send = yield send
    keep, come = keep.reshape(shape), core_swap(send).reshape(shape)
    for bit, first in ((first_bit, True), (second_bit, False)):
        send = yield add(pick(keep, 1 - bit, 1), pick(come, 1 - bit, 1))
        keep, come = add(pick(keep, bit, 1), pick(come, bit, 1)), ring_swap(send, first_axis, first)
    keep, come = (a.reshape((4,) + shape[4:]) for a in (keep, come))

    def two(which_half, which_near):
        index = [jnp.where(core == 0, which_half * 2 + i, i * 2 + which_near) for i in range(2)]
        return jnp.stack([add(pick(keep, i, 0), pick(come, i, 0)) for i in index])

    send = yield two(1 - half, 1 - near)
    keep, come = two(half, near), depth_swap(send, True)
    bit = jnp.where(core == 0, near, half)
    send = yield add(pick(keep, 1 - bit, 0), pick(come, 1 - bit, 0))
    keep, come = add(pick(keep, bit, 0), pick(come, bit, 0)), depth_swap(send, False)
    for first in (True, False):
        send = yield add(keep, come)
        keep, come = send, ring_swap(send, last_axis, first)
    send = yield add(keep, come)
    send = yield ordered(send, lax.ppermute(send, NEAR, SWAP), near, 0)
    send = yield ordered(send, ring_swap(send, first_axis, False), second_bit, 0)
    come = yield ring_swap(send, first_axis, True)
    send = yield ordered(send, come, first_bit, 0)
    yield send, core_swap(send)


def local(tokens, norm_gain_one, qkv_weight, attn_out_weight, norm_gain_two, in_weight, mlp_out_weight, cotangent):
    core, half = lax.axis_index(CORE), lax.axis_index(FAR)
    where = jnp.stack([half, core]).astype(jnp.int32)
    block = across_halves(block_of(qkv_weight))
    in_own = block_of(in_weight)
    rest_own = jnp.concatenate(
        [block_of(attn_out_weight), block_of(mlp_out_weight)] + [in_own[:, n * 768 : (n + 1) * 768] for n in range(3)], 0
    )
    edge = jnp.where(half == 0, tokens[ROWS - HALF_WIN :], tokens[:HALF_WIN])
    gains = jnp.pad(jnp.stack([norm_gain_one, norm_gain_two]), ((0, 14), (0, 384)))
    edge, rest_own = together(jnp.concatenate([edge, gains], 0), rest_own)
    beside = lax.ppermute(edge, FAR, SWAP)
    block, rest_own, beside = together(block, rest_own, beside)
    rest = across_halves(rest_own)
    both = beside_x(block, ring_swap(block, XAXIS, True))
    qkv = (qkv_weight, both, core_swap(both))
    fetched = beside[HALF_WIN:, :384]
    beside = beside[:HALF_WIN]
    gain_one = ordered(norm_gain_one, fetched[0], half, 0).reshape(1, 768).astype(F32)
    gain_two = ordered(norm_gain_two, fetched[1], half, 0).reshape(1, 768).astype(F32)
    index = jnp.arange(ROWS + HALF_WIN, dtype=jnp.int32)
    position = jnp.where(index < ROWS, half * ROWS + index, jnp.where(half == 0, index, index - HALF_WIN))
    lane = jnp.arange(128, dtype=jnp.int32)
    frequency = theta ** (-((lane % 32).astype(F32) * 2.0 / HEAD_DIM))
    angles = position.astype(F32)[:, None] * frequency[None, :]
    cosine = jnp.cos(angles)
    sine = jnp.where((lane % HEAD_DIM) < HEAD_DIM // 2, -1.0, 1.0) * jnp.sin(angles)

    h = lambda arrays: [(a, "h") for a in arrays]
    v = lambda *arrays: [(a, "v") for a in arrays]
    s = [(where, "s")]
    dma = pltpu.SemaphoreType.DMA
    wide, narrow, tall = pltpu.VMEM((768, 2304), BF16), pltpu.VMEM((768, 768), BF16), pltpu.VMEM((1152, 768), BF16)
    normed, query, key, value = run(
        qkv_kernel, s + v(tokens, beside, gain_one, cosine, sine) + h(qkv),
        [((ROWS + HALF_WIN, 768), BF16), ((ROWS, 768), BF16), ((640, 768), BF16), ((640, 768), BF16)],
        [wide, dma((5,))], 2 * 576 * 768 * 2304,
    )
    query, rest = together(query, rest)
    attended, probs = run(
        attend_kernel, s + v(query, key, value),
        [((ROWS, 768), BF16), ((4, 6, 256, 256), BF16)], [], 2 * 512 * 768 * 1024,
    )
    attended, come = together(attended, ring_swap(rest, XAXIS, True))
    both = beside_x(rest, come)
    rest = [both, core_swap(both)]
    hidden, d_up, send, keep, layer_output = run(
        mlp_kernel,
        s + v(attended, tokens, gain_two, cotangent) + h([attn_out_weight, in_weight, mlp_out_weight] + rest),
        [((ROWS, 768), F32), ((ROWS, 2 * FF), BF16), ((2, 4, 432, 384), BF16), ((2, 4, 432, 384), BF16),
         ((ROWS, 768), BF16)],
        [narrow, wide, tall, pltpu.VMEM((ROWS, 768), BF16), pltpu.VMEM((ROWS, FF), BF16),
         pltpu.VMEM((ROWS, 384), F32), pltpu.VMEM((ROWS, 384), F32), pltpu.VMEM((ROWS, 384), F32), dma((3, 13))],
        2 * 512 * 768 * 6600,
    )
    early = total_rows(send, keep, (2, 2, 2, 2, 216, 384), YAXIS, XAXIS)
    early_next = early.send(early.send(None))
    (d_hidden,) = run(
        mlp_back_kernel, s + v(d_up, hidden, cotangent, gain_two) + h([in_weight] + rest),
        [((ROWS, 768), F32)], [wide, pltpu.VMEM((ROWS, 768), F32), dma((13,))], 2 * 512 * 768 * 2304,
    )
    early_sent, d_hidden = together(early_next, d_hidden)
    early_next = early.send(early_sent)
    d_projected, edge_grad, send, keep = run(
        attend_back_kernel,
        s + v(d_hidden, query, key, value, probs, cosine, sine, attended, normed) + h([attn_out_weight] + rest),
        [((ROWS, 2304), BF16), ((HALF_WIN, 1536), BF16), ((2, 4, 384, 384), BF16), ((2, 4, 384, 384), BF16)],
        [narrow, pltpu.VMEM((ROWS, 768), BF16), pltpu.VMEM((ROWS, 768), BF16), pltpu.VMEM((640, 768), F32),
         pltpu.VMEM((640, 768), F32), pltpu.VMEM((ROWS + HALF_WIN, 2304), BF16), dma((5,))],
        2 * 512 * 768 * (768 + 2048 + 2304 + 768),
    )
    late = total_rows(send, keep, (2, 2, 2, 2, 192, 384), XAXIS, YAXIS)
    late_sent, early_sent = together(late.send(None), early_next)
    edge_grad = lax.ppermute(edge_grad, FAR, SWAP)
    late_sent, early_next = late.send(late_sent), early.send(early_sent)
    (token_grad,) = run(
        token_grad_kernel, s + v(tokens, gain_one, d_projected, edge_grad, d_hidden) + h(qkv),
        [((ROWS, 768), BF16)],
        [wide, pltpu.VMEM((ROWS, 768), F32), dma((5,))], 2 * 512 * 768 * 2304,
    )
    late_next, early_next, token_grad = together(late.send(late_sent), early_next, token_grad)
    while not isinstance(early_next, tuple):
        early_next = early.send(early_next)

    def finish(pair, weight, gain, rows):
        return run(
            finish_kernel,
            s + v(*(a.reshape(4, -1, 384) for a in pair), weight, gain.reshape(1, 384)),
            [((384, 2304), F32), ((rows, 768), F32), ((384,), F32)], [], 0,
        )

    for _ in range(9):
        late_next = late.send(late_next)
    late_next, early_mine, early_other = together(late_next, *early_next)
    in_sum, mlp_out_sum, gain_two_sum = finish((early_mine, early_other), in_weight, norm_gain_two, 576)
    late_next = late.send(late_next)
    qkv_sum, attn_out_sum, gain_one_sum = finish(late_next, qkv_weight, norm_gain_one, 384)
    return (
        layer_output,
        token_grad,
        gain_one_sum,
        qkv_sum,
        attn_out_sum,
        gain_two_sum,
        in_sum,
        mlp_out_sum,
    )


def solution(mesh):
    fine = jax.sharding.Mesh(
        mesh.devices.reshape(4, 4, 2, 2, 2), (YAXIS, XAXIS, NEAR, CORE, FAR)
    )
    every = P((YAXIS, XAXIS, NEAR, CORE, FAR), None)
    return jax.shard_map(
        local,
        mesh=fine,
        in_specs=(every, P(FAR), P(FAR, None), P(FAR, None), P(FAR), P(FAR, None), P(FAR, None), every),
        out_specs=(every, every, P(FAR), P(FAR, None), P(FAR, None), P(FAR), P(FAR, None), P(FAR, None)),
        check_vma=False,
    )
```

```python
import math

import jax
import jax.numpy as jnp
from jax import lax
from jax.experimental import pallas as pl
from jax.experimental.pallas import tpu as pltpu
from jax.sharding import PartitionSpec as P

HEADS = 12
HEAD_DIM = 64
FF = 1152
HALF_WIN = 64
TILE = 2 * HALF_WIN
ROWS = 512
F32, BF16 = jnp.float32, jnp.bfloat16

eps_norm = 1e-05
theta = 10000.0
masked_value = -1e30

YAXIS, XAXIS, NEAR, CORE, FAR = "y", "x", "zl", "c", "zh"
PAIRS_A = [(0, 1), (1, 0), (2, 3), (3, 2)]
PAIRS_B = [(0, 3), (3, 0), (1, 2), (2, 1)]
SWAP = [(0, 1), (1, 0)]


def ring_swap(x, axis, first):
    even, odd = (PAIRS_A, PAIRS_B) if first else (PAIRS_B, PAIRS_A)
    if axis == YAXIS:
        pairs = [
            ((i * 4 + k) * 4 + r, (j * 4 + k) * 4 + r)
            for z in range(2)
            for c, group in ((0, even), (1, odd))
            for r in (z * 2 + c,)
            for k in range(4)
            for i, j in group
        ]
        return lax.ppermute(x, (YAXIS, XAXIS, NEAR, CORE), pairs)
    pairs = [
        (i * 4 + z * 2 + c, j * 4 + z * 2 + c)
        for z in range(2)
        for c, group in ((0, even), (1, odd))
        for i, j in group
    ]
    return lax.ppermute(x, (XAXIS, NEAR, CORE), pairs)


def depth_swap(x, first):
    across = [(i, 3 - i) for i in range(4)]
    within = [(i, i ^ 2) for i in range(4)]
    even, odd = (across, within) if first else (within, across)
    pairs = []
    for c, group in ((0, even), (1, odd)):
        for i, j in group:
            pairs.append(((i >> 1) * 4 + c * 2 + (i & 1), (j >> 1) * 4 + c * 2 + (j & 1)))
    return lax.ppermute(x, (NEAR, CORE, FAR), pairs)


def across_halves(x):
    return lax.ppermute(x, (NEAR, FAR), [(i, 3 - i) for i in range(4)])


def core_swap(x):
    return lax.ppermute(x, CORE, SWAP)


def pick(x, index, axis):
    return lax.dynamic_index_in_dim(x, index, axis, keepdims=False)


def ordered(mine, other, index, axis):
    return jnp.where(index == 0, jnp.stack([mine, other], axis), jnp.stack([other, mine], axis))


def add(a, b):
    return (a.astype(jnp.float32) + b.astype(jnp.float32)).astype(jnp.bfloat16)


def ln_stats(v):
    mean = jnp.mean(v, axis=-1, keepdims=True)
    centred = v - mean
    scale = lax.rsqrt(jnp.mean(centred * centred, axis=-1, keepdims=True) + eps_norm)
    return centred * scale, scale


def ln_back(grad, gain, normal, scale):
    inner = grad * gain
    mean_inner = jnp.mean(inner, axis=-1, keepdims=True)
    mean_cross = jnp.mean(inner * normal, axis=-1, keepdims=True)
    return scale * (inner - mean_inner - normal * mean_cross)


def mm(a, b):
    return jnp.dot(a, b, preferred_element_type=F32)


def mm_nt(a, b):
    return lax.dot_general(a, b, (((1,), (1,)), ((), ())), preferred_element_type=F32)


def mm_tn(a, b):
    return lax.dot_general(a, b, (((0,), (0,)), ((), ())), preferred_element_type=F32)


def rows_loop(rows, chunk, body):
    def step(i, carry):
        body(pl.ds(pl.multiple_of(i * chunk, chunk), chunk))
        return carry

    lax.fori_loop(0, rows // chunk, step, 0)


def place_weight(where_ref, pieces, full, sems, skip=0, parts=1):
    half, core = where_ref[0], where_ref[1]
    own, mine, others = pieces
    rows, cols = own.shape[0], own.shape[1] // parts
    block = rows // 4
    other = (1 - half) * rows
    copies = [pltpu.make_async_copy(own, full.at[pl.ds(pl.multiple_of(half * rows, 16), rows)], sems.at[0])]
    for source, which in ((mine, core), (others, 1 - core)):
        for b in range(2):
            place = pl.ds(pl.multiple_of(other + (which * 2 + b) * block, 16), block)
            for j in range(parts):
                copies.append(
                    pltpu.make_async_copy(
                        source.at[b, pl.ds(skip + j * block, block)],
                        full.at[place, pl.ds(j * cols, cols)],
                        sems.at[len(copies)],
                    )
                )
    for copy in copies:
        copy.start()
    return copies


def turned(tile, lane):
    return jnp.where(lane, pltpu.roll(tile, 96, 1), pltpu.roll(tile, 32, 1))


def low_lanes(rows, period):
    lanes = lax.broadcasted_iota(jnp.int32, (rows, 128), 1)
    return (lanes % period) < period // 2


def qkv_kernel(where_ref, x_ref, beside_ref, gain_ref, cos_ref, sin_ref, own, first, second,
               normed_out, query_out, key_out, value_out, full, sems):
    copies = place_weight(where_ref, (own, first, second), full, sems)
    normed, query_ref, key_ref, value_ref = (out.ref for out in (normed_out, query_out, key_out, value_out))
    gain, x_ref, beside_ref = gain_ref()[...], x_ref(), beside_ref()

    def main(rows):
        normal, _ = ln_stats(x_ref[rows, :].astype(F32))
        normed[rows, :] = (normal * gain).astype(BF16)

    rows_loop(ROWS, 128, main)
    normal, _ = ln_stats(beside_ref[...].astype(F32))
    normed[ROWS:, :] = (normal * gain).astype(BF16)
    normed_out.send()
    for copy in copies:
        copy.wait()
    cos_ref, sin_ref = cos_ref(), sin_ref()
    lane = low_lanes(ROWS + HALF_WIN, HEAD_DIM)
    for j in range(9):
        cols = slice(j * 256, (j + 1) * 256)
        proj = mm(normed[...], full[:, cols])
        for side in range(2):
            tile = proj[:, side * 128 : (side + 1) * 128]
            if j < 6:
                tile = tile * cos_ref[...] + turned(tile, lane) * sin_ref[...]
            place = slice((j % 3) * 256 + side * 128, (j % 3) * 256 + (side + 1) * 128)
            if j < 3:
                query_ref[:, place] = (tile[:ROWS] * 0.125).astype(BF16)
            else:
                out_ref = key_ref if j < 6 else value_ref
                edge = tile[ROWS:].astype(BF16)
                out_ref[HALF_WIN : HALF_WIN + ROWS, place] = tile[:ROWS].astype(BF16)
                out_ref[:HALF_WIN, place] = edge
                out_ref[HALF_WIN + ROWS :, place] = edge
        if j == 2:
            query_out.send()
        if j == 5:
            key_out.send()


def attend_kernel(where_ref, q_ref, k_ref, v_ref, att_out, prob_out):
    att_ref, prob_ref = att_out.ref, prob_out.ref
    q_ref, k_ref, v_ref = q_ref(), k_ref(), v_ref()
    half = where_ref[0]
    low_q, low_k = low_lanes(TILE, 128), low_lanes(2 * TILE, 128)
    row = lax.broadcasted_iota(jnp.int32, (2 * TILE, 2 * TILE), 0) % TILE
    col = lax.broadcasted_iota(jnp.int32, (2 * TILE, 2 * TILE), 1)
    band = (col >= row) & (col <= row + 2 * HALF_WIN)

    def tile_step(t, carry):
        begin = jnp.where((half == 0) & (t == 0), HALF_WIN, 0)
        end = jnp.where((half == 1) & (t == ROWS // TILE - 1), 2 * TILE - HALF_WIN, 2 * TILE)
        allowed = band & (col >= begin) & (col < end)
        rows = pl.ds(pl.multiple_of(t * TILE, TILE), TILE)
        span = pl.ds(pl.multiple_of(t * TILE, TILE), 2 * TILE)
        for pair in range(HEADS // 2):
            lanes = slice(pair * 128, (pair + 1) * 128)
            q = q_ref[rows, lanes]
            zero = jnp.zeros_like(q)
            stacked = jnp.concatenate([jnp.where(low_q, q, zero), jnp.where(low_q, zero, q)], 0)
            scores = jnp.where(allowed, mm_nt(stacked, k_ref[span, lanes]), masked_value)
            raised = jnp.exp(scores - jnp.max(scores, axis=-1, keepdims=True))
            probs = (raised / jnp.sum(raised, axis=-1, keepdims=True)).astype(BF16)
            prob_ref[t, pair] = probs
            v = v_ref[span, lanes]
            none = jnp.zeros_like(v)
            att_ref[rows, lanes] = mm(
                jnp.concatenate([probs[:TILE], probs[TILE:]], 1),
                jnp.concatenate([jnp.where(low_k, v, none), jnp.where(low_k, none, v)], 0),
            ).astype(BF16)
        return carry

    lax.fori_loop(0, ROWS // TILE, tile_step, 0)


def mlp_kernel(where_ref, att_ref, x_ref, gain_ref, cot_ref, att_own, in_own, out_own, first, second,
               hidden_out, up_out, send_out, keep_out, layer_out,
               w_att, w_in, w_out, normed, mixed, act_s, gate_s, dmix_s, sems):
    att_copies = place_weight(where_ref, (att_own, first, second), w_att, sems.at[0])
    in_copies = place_weight(where_ref, (in_own, first, second), w_in, sems.at[1], 240, 3)
    out_copies = place_weight(where_ref, (out_own, first, second), w_out, sems.at[2], 96)
    core = where_ref[1]
    hidden_ref, d_up, layer_ref = hidden_out.ref, up_out.ref, layer_out.ref
    att_ref, x_ref, gain = att_ref(), x_ref(), gain_ref()[...]
    for copy in att_copies:
        copy.wait()
    for j in range(3):
        cols = slice(j * 256, (j + 1) * 256)
        hidden_ref[:, cols] = x_ref[:, cols].astype(F32) + mm(att_ref[...], w_att[:, cols])
    hidden_out.send()

    def normalize(rows):
        normal, _ = ln_stats(hidden_ref[rows, :])
        normed[rows, :] = (normal * gain).astype(BF16)

    rows_loop(ROWS, 128, normalize)
    cot_ref = cot_ref()
    for copy in in_copies + out_copies:
        copy.wait()
    for j in range(3):
        cols = slice(j * 384, (j + 1) * 384)
        gates = slice(FF + j * 384, FF + (j + 1) * 384)
        act_s[...] = mm(normed[...], w_in[:, cols])
        gate_s[...] = mm(normed[...], w_in[:, gates])
        dmix_s[...] = mm_nt(cot_ref[...], w_out[cols, :])

        def gate(rows):
            act, gated_by, d_mixed = act_s[rows, :], gate_s[rows, :], dmix_s[rows, :]
            cumulative = 0.5 * (1.0 + lax.erf(act * 0.7071067811865476))
            density = jnp.exp(-0.5 * act * act) * 0.3989422804014327
            curved = act * cumulative
            mixed[rows, cols] = (curved * gated_by).astype(BF16)
            d_up[rows, cols] = (d_mixed * gated_by * (cumulative + act * density)).astype(BF16)
            d_up[rows, gates] = (d_mixed * curved).astype(BF16)

        rows_loop(ROWS, 128, gate)
    up_out.send()
    for out, which in ((send_out, 1 - core), (keep_out, core)):
        for j in range(3):
            cols = pl.ds(pl.multiple_of(which * 1152 + j * 384, 128), 384)
            grad = mm_tn(normed[...], d_up[:, cols]).astype(BF16)
            out.ref[:, :, j * 96 : (j + 1) * 96] = grad.reshape(2, 4, 96, 384)
        cols = pl.ds(pl.multiple_of(which * 384, 128), 384)
        grad = mm_tn(mixed[...], cot_ref[:, cols]).astype(BF16)
        out.ref[:, :, 288:] = grad.reshape(2, 4, 144, 384)
        out.send()
    for j in range(3):
        cols = slice(j * 256, (j + 1) * 256)
        layer_ref[:, cols] = (hidden_ref[:, cols] + mm(mixed[...], w_out[:, cols])).astype(BF16)


def mlp_back_kernel(where_ref, up_ref, hidden_ref, cot_ref, gain_ref, in_own, first, second,
                    dhid_out, w_in, dnorm_s, sems):
    copies = place_weight(where_ref, (in_own, first, second), w_in, sems, 240, 3)
    d_up = up_ref()
    for copy in copies:
        copy.wait()
    for j in range(3):
        cols = slice(j * 256, (j + 1) * 256)
        dnorm_s[:, cols] = mm_nt(d_up[...], w_in[cols, :])
    hidden_ref, cot_ref, gain = hidden_ref(), cot_ref(), gain_ref()[...]

    def back(rows):
        normal, scale = ln_stats(hidden_ref[rows, :])
        dhid_out.ref[rows, :] = cot_ref[rows, :].astype(F32) + ln_back(dnorm_s[rows, :], gain, normal, scale)

    rows_loop(ROWS, 128, back)


def attend_back_kernel(where_ref, dhid_ref, q_ref, k_ref, v_ref, prob_ref, cos_ref, sin_ref, att_ref, normed_ref,
                       own, first, second, dproj_out, edge_out, send_out, keep_out,
                       full, branch, datt, dkey, dvalue, grads_s, sems):
    copies = place_weight(where_ref, (own, first, second), full, sems)
    half, core = where_ref[0], where_ref[1]
    dproj_ref, edge_ref = dproj_out.ref, edge_out.ref
    dkey[...] = jnp.zeros_like(dkey)
    dvalue[...] = jnp.zeros_like(dvalue)
    for copy in copies:
        copy.wait()
    branch[...] = dhid_ref()[...].astype(BF16)
    for j in range(3):
        cols = slice(j * 256, (j + 1) * 256)
        datt[:, cols] = mm_nt(branch[...], full[cols, :]).astype(BF16)
    q_ref, k_ref, v_ref, prob_ref, cos_ref, sin_ref = (
        ref() for ref in (q_ref, k_ref, v_ref, prob_ref, cos_ref, sin_ref)
    )
    low_q, low_k = low_lanes(TILE, 128), low_lanes(2 * TILE, 128)
    turn_q = low_lanes(TILE, HEAD_DIM)

    def split(tile, low, axis=0):
        none = jnp.zeros_like(tile)
        return jnp.concatenate([jnp.where(low, tile, none), jnp.where(low, none, tile)], axis)

    def tile_step(t, carry):
        rows = pl.ds(pl.multiple_of(t * TILE, TILE), TILE)
        span = pl.ds(pl.multiple_of(t * TILE, TILE), 2 * TILE)
        cos, sin = cos_ref[rows, :], sin_ref[rows, :]
        for pair in range(HEADS // 2):
            lanes = slice(pair * 128, (pair + 1) * 128)
            grads = split(datt[rows, lanes], low_q)
            probs_b = prob_ref[t, pair]
            probs = probs_b.astype(F32)
            d_probs = mm_nt(grads, v_ref[span, lanes])
            delta = jnp.sum(probs * d_probs, axis=-1, keepdims=True)
            d_scores = (probs * (d_probs - delta)).astype(BF16)
            d_query = 0.125 * mm(
                jnp.concatenate([d_scores[:TILE], d_scores[TILE:]], 1), split(k_ref[span, lanes], low_k)
            )
            dproj_ref[rows, lanes] = (d_query * cos - turned(d_query, turn_q) * sin).astype(BF16)
            dkey[span, lanes] += mm_tn(d_scores, split(q_ref[rows, lanes], low_q))
            dvalue[span, lanes] += mm_tn(probs_b, grads)
        return carry

    lax.fori_loop(0, ROWS // TILE, tile_step, 0)
    turn_k = low_lanes(ROWS, HEAD_DIM)
    turn_e = low_lanes(HALF_WIN, HEAD_DIM)
    edge = pl.ds(pl.multiple_of((1 - half) * (ROWS + HALF_WIN), HALF_WIN), HALF_WIN)
    for pair in range(HEADS // 2):
        lanes = slice(pair * 128, (pair + 1) * 128)
        tile = dkey[HALF_WIN : HALF_WIN + ROWS, lanes]
        dproj_ref[:, 768 + pair * 128 : 768 + (pair + 1) * 128] = (
            tile * cos_ref[:ROWS] - turned(tile, turn_k) * sin_ref[:ROWS]
        ).astype(BF16)
        dproj_ref[:, 1536 + pair * 128 : 1536 + (pair + 1) * 128] = dvalue[
            HALF_WIN : HALF_WIN + ROWS, lanes
        ].astype(BF16)
        tile = dkey[edge, lanes]
        edge_ref[:, lanes] = (tile * cos_ref[ROWS:] - turned(tile, turn_e) * sin_ref[ROWS:]).astype(BF16)
        edge_ref[:, 768 + pair * 128 : 768 + (pair + 1) * 128] = dvalue[edge, lanes].astype(BF16)
    edge_out.send()
    dproj_out.send()
    normed_ref, att_ref = normed_ref(), att_ref()
    grads_s[:ROWS, :] = dproj_ref[...]
    grads_s[ROWS:, :768] = jnp.zeros((HALF_WIN, 768), BF16)
    grads_s[ROWS:, 768:] = edge_ref[...]
    for out, which in ((send_out, 1 - core), (keep_out, core)):
        for j in range(3):
            cols = pl.ds(pl.multiple_of(which * 1152 + j * 384, 128), 384)
            grad = mm_tn(normed_ref[...], grads_s[:, cols]).astype(BF16)
            out.ref[:, :, j * 96 : (j + 1) * 96] = grad.reshape(2, 4, 96, 384)
        cols = pl.ds(pl.multiple_of(which * 384, 128), 384)
        grad = mm_tn(att_ref[...], branch[:, cols]).astype(BF16)
        out.ref[:, :, 288:] = grad.reshape(2, 4, 96, 384)
        out.send()


def token_grad_kernel(where_ref, x_ref, gain_ref, dproj_ref, edge_ref, dhid_ref, own, first, second,
                      out, full, dnorm, sems):
    copies = place_weight(where_ref, (own, first, second), full, sems)
    grads, edge_ref = dproj_ref(), edge_ref()
    edge = pl.ds(pl.multiple_of((1 - where_ref[0]) * (ROWS - HALF_WIN), HALF_WIN), HALF_WIN)
    grads[edge, 768:] = (grads[edge, 768:].astype(F32) + edge_ref[...].astype(F32)).astype(BF16)
    for copy in copies:
        copy.wait()
    for j in range(3):
        cols = slice(j * 256, (j + 1) * 256)
        dnorm[:, cols] = mm_nt(grads[...], full[cols, :])

    gain, x_ref, dhid_ref = gain_ref()[...], x_ref(), dhid_ref()

    def back(rows):
        normal, scale = ln_stats(x_ref[rows, :].astype(F32))
        out.ref[rows, :] = (dhid_ref[rows, :] + ln_back(dnorm[rows, :], gain, normal, scale)).astype(BF16)

    rows_loop(ROWS, 128, back)


def finish_kernel(where_ref, mine, other, weight, gain, wide_out, narrow_out, gain_out):
    core = where_ref[1]
    wide_ref, narrow_ref = wide_out.ref, narrow_out.ref
    rows = narrow_ref.shape[0]
    for staged, which in ((mine, core), (other, 1 - core)):
        source = staged()
        for j in range(3):
            cols = pl.ds(pl.multiple_of(which * 1152 + j * 384, 128), 384)
            wide_ref[:, cols] = source[:, j * 96 : (j + 1) * 96].reshape(384, 384).astype(F32)
        cols = pl.ds(pl.multiple_of(which * 384, 128), 384)
        narrow_ref[:, cols] = source[:, 288:].reshape(rows, 384).astype(F32)
    wide_out.send()
    narrow_out.send()
    gain_rows(wide_ref, weight(), gain(), gain_out.ref)


def gain_rows(grad_ref, weight, gain, gain_ref):
    for n in range(3):
        rows = slice(n * 128, (n + 1) * 128)
        total = jnp.sum(grad_ref[rows, :] * weight[rows, :].astype(F32), axis=-1, keepdims=True)
        gain_ref[rows] = (jnp.broadcast_to(total, (128, 128)).T[:1] / gain[:, rows].astype(F32))[0]


class Staged:
    def __init__(self, source, ref, sem):
        self.ref, self.copy, self.there = ref, pltpu.make_async_copy(source, ref, sem), False
        self.copy.start()

    def __call__(self):
        if not self.there:
            self.copy.wait()
            self.there = True
        return self.ref


class Result:
    def __init__(self, ref, target, sem):
        self.ref, self.copy, self.sent = ref, pltpu.make_async_copy(ref, target, sem), False

    def send(self):
        if not self.sent:
            self.copy.start()
            self.sent = True


def run(kernel, ins, outs, scratch, flops):
    staged = [a for a, kind in ins if kind == "v"]
    spaces = {"s": pltpu.SMEM, "h": pl.ANY, "v": pl.ANY}
    moved = sum(a.size * a.dtype.itemsize for a, _ in ins) + sum(
        math.prod(shape) * jnp.dtype(dtype).itemsize for shape, dtype in outs
    )

    def body(*refs):
        given, refs = refs[: len(ins)], refs[len(ins) :]
        targets, refs = refs[: len(outs)], refs[len(outs) :]
        places, refs = refs[: len(staged)], refs[len(staged) :]
        ready, refs = refs[: len(outs)], refs[len(outs) :]
        in_sems, out_sems, *rest = refs
        taken, n = [], 0
        for ref, (_, kind) in zip(given, ins):
            if kind == "v":
                ref = Staged(ref, places[n], in_sems.at[n])
                n += 1
            taken.append(ref)
        results = [Result(r, t, out_sems.at[k]) for k, (r, t) in enumerate(zip(ready, targets))]
        kernel(*taken, *results, *rest)
        for ref in taken:
            if isinstance(ref, Staged):
                ref()
        for result in results:
            result.send()
        for result in results:
            result.copy.wait()

    dma = pltpu.SemaphoreType.DMA
    return pl.pallas_call(
        body,
        in_specs=[pl.BlockSpec(memory_space=spaces[kind]) for _, kind in ins],
        out_specs=[pl.BlockSpec(memory_space=pl.ANY) for _ in outs],
        out_shape=[jax.ShapeDtypeStruct(shape, dtype) for shape, dtype in outs],
        scratch_shapes=[pltpu.VMEM(a.shape, a.dtype) for a in staged]
        + [pltpu.VMEM(shape, dtype) for shape, dtype in outs]
        + [dma((len(staged),)), dma((len(outs),))]
        + scratch,
        compiler_params=pltpu.CompilerParams(vmem_limit_bytes=60 * 1024 * 1024),
        cost_estimate=pl.CostEstimate(flops=int(flops), bytes_accessed=int(moved), transcendentals=0),
    )(*[a for a, _ in ins])


def together(*arrays):
    return lax.optimization_barrier(arrays)


def block_of(own):
    rows, cols = own.shape
    index = lax.axis_index(CORE) * 2 + (lax.axis_index(XAXIS) & 1)
    return pick(own.reshape(4, rows // 4, cols), index, 0)


def beside_x(block, come):
    return ordered(block, come, lax.axis_index(XAXIS) & 1, 0)


def total_rows(send, keep, shape, first_axis, last_axis):
    core, half = lax.axis_index(CORE), lax.axis_index(FAR)
    near, place = lax.axis_index(NEAR) ^ half, lax.axis_index(first_axis)
    first_bit = jnp.where(core == 0, ((place + 1) >> 1) & 1, place >> 1)
    second_bit = place & 1
    send = yield send
    keep, come = keep.reshape(shape), core_swap(send).reshape(shape)
    for bit, first in ((first_bit, True), (second_bit, False)):
        send = yield add(pick(keep, 1 - bit, 1), pick(come, 1 - bit, 1))
        keep, come = add(pick(keep, bit, 1), pick(come, bit, 1)), ring_swap(send, first_axis, first)
    keep, come = (a.reshape((4,) + shape[4:]) for a in (keep, come))

    def two(which_half, which_near):
        index = [jnp.where(core == 0, which_half * 2 + i, i * 2 + which_near) for i in range(2)]
        return jnp.stack([add(pick(keep, i, 0), pick(come, i, 0)) for i in index])

    send = yield two(1 - half, 1 - near)
    keep, come = two(half, near), depth_swap(send, True)
    bit = jnp.where(core == 0, near, half)
    send = yield add(pick(keep, 1 - bit, 0), pick(come, 1 - bit, 0))
    keep, come = add(pick(keep, bit, 0), pick(come, bit, 0)), depth_swap(send, False)
    for first in (True, False):
        send = yield add(keep, come)
        keep, come = send, ring_swap(send, last_axis, first)
    send = yield add(keep, come)
    send = yield ordered(send, lax.ppermute(send, NEAR, SWAP), near, 0)
    send = yield ordered(send, ring_swap(send, first_axis, False), second_bit, 0)
    come = yield ring_swap(send, first_axis, True)
    send = yield ordered(send, come, first_bit, 0)
    yield send, core_swap(send)


def local(tokens, norm_gain_one, qkv_weight, attn_out_weight, norm_gain_two, in_weight, mlp_out_weight, cotangent):
    core, half = lax.axis_index(CORE), lax.axis_index(FAR)
    where = jnp.stack([half, core]).astype(jnp.int32)
    block = across_halves(block_of(qkv_weight))
    in_own = block_of(in_weight)
    rest_own = jnp.concatenate(
        [block_of(attn_out_weight), block_of(mlp_out_weight)] + [in_own[:, n * 768 : (n + 1) * 768] for n in range(3)], 0
    )
    edge = jnp.where(half == 0, tokens[ROWS - HALF_WIN :], tokens[:HALF_WIN])
    gains = jnp.pad(jnp.stack([norm_gain_one, norm_gain_two]), ((0, 14), (0, 384)))
    edge, rest_own = together(jnp.concatenate([edge, gains], 0), rest_own)
    beside = lax.ppermute(edge, FAR, SWAP)
    block, rest_own, beside = together(block, rest_own, beside)
    rest = across_halves(rest_own)
    both = beside_x(block, ring_swap(block, XAXIS, True))
    qkv = (qkv_weight, both, core_swap(both))
    fetched = beside[HALF_WIN:, :384]
    beside = beside[:HALF_WIN]
    gain_one = ordered(norm_gain_one, fetched[0], half, 0).reshape(1, 768).astype(F32)
    gain_two = ordered(norm_gain_two, fetched[1], half, 0).reshape(1, 768).astype(F32)
    index = jnp.arange(ROWS + HALF_WIN, dtype=jnp.int32)
    position = jnp.where(index < ROWS, half * ROWS + index, jnp.where(half == 0, index, index - HALF_WIN))
    lane = jnp.arange(128, dtype=jnp.int32)
    frequency = theta ** (-((lane % 32).astype(F32) * 2.0 / HEAD_DIM))
    angles = position.astype(F32)[:, None] * frequency[None, :]
    cosine = jnp.cos(angles)
    sine = jnp.where((lane % HEAD_DIM) < HEAD_DIM // 2, -1.0, 1.0) * jnp.sin(angles)

    h = lambda arrays: [(a, "h") for a in arrays]
    v = lambda *arrays: [(a, "v") for a in arrays]
    s = [(where, "s")]
    dma = pltpu.SemaphoreType.DMA
    wide, narrow, tall = pltpu.VMEM((768, 2304), BF16), pltpu.VMEM((768, 768), BF16), pltpu.VMEM((1152, 768), BF16)
    normed, query, key, value = run(
        qkv_kernel, s + v(tokens, beside, gain_one, cosine, sine) + h(qkv),
        [((ROWS + HALF_WIN, 768), BF16), ((ROWS, 768), BF16), ((640, 768), BF16), ((640, 768), BF16)],
        [wide, dma((5,))], 2 * 576 * 768 * 2304,
    )
    query, rest = together(query, rest)
    attended, probs = run(
        attend_kernel, s + v(query, key, value),
        [((ROWS, 768), BF16), ((4, 6, 256, 256), BF16)], [], 2 * 512 * 768 * 1024,
    )
    attended, come = together(attended, ring_swap(rest, XAXIS, True))
    both = beside_x(rest, come)
    rest = [both, core_swap(both)]
    hidden, d_up, send, keep, layer_output = run(
        mlp_kernel,
        s + v(attended, tokens, gain_two, cotangent) + h([attn_out_weight, in_weight, mlp_out_weight] + rest),
        [((ROWS, 768), F32), ((ROWS, 2 * FF), BF16), ((2, 4, 432, 384), BF16), ((2, 4, 432, 384), BF16),
         ((ROWS, 768), BF16)],
        [narrow, wide, tall, pltpu.VMEM((ROWS, 768), BF16), pltpu.VMEM((ROWS, FF), BF16),
         pltpu.VMEM((ROWS, 384), F32), pltpu.VMEM((ROWS, 384), F32), pltpu.VMEM((ROWS, 384), F32), dma((3, 13))],
        2 * 512 * 768 * 6600,
    )
    early = total_rows(send, keep, (2, 2, 2, 2, 216, 384), YAXIS, XAXIS)
    early_next = early.send(early.send(None))
    (d_hidden,) = run(
        mlp_back_kernel, s + v(d_up, hidden, cotangent, gain_two) + h([in_weight] + rest),
        [((ROWS, 768), F32)], [wide, pltpu.VMEM((ROWS, 768), F32), dma((13,))], 2 * 512 * 768 * 2304,
    )
    early_sent, d_hidden = together(early_next, d_hidden)
    early_next = early.send(early_sent)
    d_projected, edge_grad, send, keep = run(
        attend_back_kernel,
        s + v(d_hidden, query, key, value, probs, cosine, sine, attended, normed) + h([attn_out_weight] + rest),
        [((ROWS, 2304), BF16), ((HALF_WIN, 1536), BF16), ((2, 4, 384, 384), BF16), ((2, 4, 384, 384), BF16)],
        [narrow, pltpu.VMEM((ROWS, 768), BF16), pltpu.VMEM((ROWS, 768), BF16), pltpu.VMEM((640, 768), F32),
         pltpu.VMEM((640, 768), F32), pltpu.VMEM((ROWS + HALF_WIN, 2304), BF16), dma((5,))],
        2 * 512 * 768 * (768 + 2048 + 2304 + 768),
    )
    late = total_rows(send, keep, (2, 2, 2, 2, 192, 384), XAXIS, YAXIS)
    late_sent, early_sent = together(late.send(None), early_next)
    edge_grad = lax.ppermute(edge_grad, FAR, SWAP)
    early_next = early.send(early_sent)
    late_sent, edge_grad = together(late.send(late_sent), edge_grad)
    (token_grad,) = run(
        token_grad_kernel, s + v(tokens, gain_one, d_projected, edge_grad, d_hidden) + h(qkv),
        [((ROWS, 768), BF16)],
        [wide, pltpu.VMEM((ROWS, 768), F32), dma((5,))], 2 * 512 * 768 * 2304,
    )
    late_next, early_next, token_grad = together(late.send(late_sent), early_next, token_grad)
    for _ in range(6):
        late_next, early_next = together(late.send(late_next), early.send(early_next))
    early_next = early.send(early.send(early_next))
    late_next, early_next = together(late.send(late_next), early_next)
    early_next = early.send(early_next)

    def finish(pair, weight, gain, rows):
        return run(
            finish_kernel,
            s + v(*(a.reshape(4, -1, 384) for a in pair), weight, gain.reshape(1, 384)),
            [((384, 2304), F32), ((rows, 768), F32), ((384,), F32)], [], 0,
        )

    for _ in range(2):
        late_next = late.send(late_next)
    late_next, early_mine, early_other = together(late_next, *early_next)
    in_sum, mlp_out_sum, gain_two_sum = finish((early_mine, early_other), in_weight, norm_gain_two, 576)
    late_next = late.send(late_next)
    qkv_sum, attn_out_sum, gain_one_sum = finish(late_next, qkv_weight, norm_gain_one, 384)
    return (
        layer_output,
        token_grad,
        gain_one_sum,
        qkv_sum,
        attn_out_sum,
        gain_two_sum,
        in_sum,
        mlp_out_sum,
    )


def solution(mesh):
    fine = jax.sharding.Mesh(
        mesh.devices.reshape(4, 4, 2, 2, 2), (YAXIS, XAXIS, NEAR, CORE, FAR)
    )
    every = P((YAXIS, XAXIS, NEAR, CORE, FAR), None)
    return jax.shard_map(
        local,
        mesh=fine,
        in_specs=(every, P(FAR), P(FAR, None), P(FAR, None), P(FAR), P(FAR, None), P(FAR, None), every),
        out_specs=(every, every, P(FAR), P(FAR, None), P(FAR, None), P(FAR), P(FAR, None), P(FAR, None)),
        check_vma=False,
    )
```

```python
import math

import jax
import jax.numpy as jnp
from jax import lax
from jax.experimental import pallas as pl
from jax.experimental.pallas import tpu as pltpu
from jax.sharding import PartitionSpec as P

HEADS = 12
HEAD_DIM = 64
FF = 1152
HALF_WIN = 64
TILE = 2 * HALF_WIN
ROWS = 512
F32, BF16 = jnp.float32, jnp.bfloat16

eps_norm = 1e-05
theta = 10000.0
masked_value = -1e30

YAXIS, XAXIS, NEAR, CORE, FAR = "y", "x", "zl", "c", "zh"
PAIRS_A = [(0, 1), (1, 0), (2, 3), (3, 2)]
PAIRS_B = [(0, 3), (3, 0), (1, 2), (2, 1)]
SWAP = [(0, 1), (1, 0)]


def ring_swap(x, axis, first):
    even, odd = (PAIRS_A, PAIRS_B) if first else (PAIRS_B, PAIRS_A)
    if axis == YAXIS:
        pairs = [
            ((i * 4 + k) * 4 + r, (j * 4 + k) * 4 + r)
            for z in range(2)
            for c, group in ((0, even), (1, odd))
            for r in (z * 2 + c,)
            for k in range(4)
            for i, j in group
        ]
        return lax.ppermute(x, (YAXIS, XAXIS, NEAR, CORE), pairs)
    pairs = [
        (i * 4 + z * 2 + c, j * 4 + z * 2 + c)
        for z in range(2)
        for c, group in ((0, even), (1, odd))
        for i, j in group
    ]
    return lax.ppermute(x, (XAXIS, NEAR, CORE), pairs)


def depth_swap(x, first):
    across = [(i, 3 - i) for i in range(4)]
    within = [(i, i ^ 2) for i in range(4)]
    even, odd = (across, within) if first else (within, across)
    pairs = []
    for c, group in ((0, even), (1, odd)):
        for i, j in group:
            pairs.append(((i >> 1) * 4 + c * 2 + (i & 1), (j >> 1) * 4 + c * 2 + (j & 1)))
    return lax.ppermute(x, (NEAR, CORE, FAR), pairs)


def across_halves(x):
    return lax.ppermute(x, (NEAR, FAR), [(i, 3 - i) for i in range(4)])


def core_swap(x):
    return lax.ppermute(x, CORE, SWAP)


def pick(x, index, axis):
    return lax.dynamic_index_in_dim(x, index, axis, keepdims=False)


def ordered(mine, other, index, axis):
    return jnp.where(index == 0, jnp.stack([mine, other], axis), jnp.stack([other, mine], axis))


def add(a, b):
    return (a.astype(jnp.float32) + b.astype(jnp.float32)).astype(jnp.bfloat16)


def ln_stats(v):
    mean = jnp.mean(v, axis=-1, keepdims=True)
    centred = v - mean
    scale = lax.rsqrt(jnp.mean(centred * centred, axis=-1, keepdims=True) + eps_norm)
    return centred * scale, scale


def ln_back(grad, gain, normal, scale):
    inner = grad * gain
    mean_inner = jnp.mean(inner, axis=-1, keepdims=True)
    mean_cross = jnp.mean(inner * normal, axis=-1, keepdims=True)
    return scale * (inner - mean_inner - normal * mean_cross)


def mm(a, b):
    return jnp.dot(a, b, preferred_element_type=F32)


def mm_nt(a, b):
    return lax.dot_general(a, b, (((1,), (1,)), ((), ())), preferred_element_type=F32)


def mm_tn(a, b):
    return lax.dot_general(a, b, (((0,), (0,)), ((), ())), preferred_element_type=F32)


def rows_loop(rows, chunk, body):
    def step(i, carry):
        body(pl.ds(pl.multiple_of(i * chunk, chunk), chunk))
        return carry

    lax.fori_loop(0, rows // chunk, step, 0)


def place_weight(where_ref, pieces, full, sems, skip=0, parts=1):
    half, core = where_ref[0], where_ref[1]
    own, mine, others = pieces
    rows, cols = own.shape[0], own.shape[1] // parts
    block = rows // 4
    other = (1 - half) * rows
    copies = [pltpu.make_async_copy(own, full.at[pl.ds(pl.multiple_of(half * rows, 16), rows)], sems.at[0])]
    for source, which in ((mine, core), (others, 1 - core)):
        for b in range(2):
            place = pl.ds(pl.multiple_of(other + (which * 2 + b) * block, 16), block)
            for j in range(parts):
                copies.append(
                    pltpu.make_async_copy(
                        source.at[b, pl.ds(skip + j * block, block)],
                        full.at[place, pl.ds(j * cols, cols)],
                        sems.at[len(copies)],
                    )
                )
    for copy in copies:
        copy.start()
    return copies


def turned(tile, lane):
    return jnp.where(lane, pltpu.roll(tile, 96, 1), pltpu.roll(tile, 32, 1))


def low_lanes(rows, period):
    lanes = lax.broadcasted_iota(jnp.int32, (rows, 128), 1)
    return (lanes % period) < period // 2


def qkv_kernel(where_ref, x_ref, beside_ref, gain_ref, cos_ref, sin_ref, own, first, second,
               normed_out, query_out, key_out, value_out, full, sems):
    copies = place_weight(where_ref, (own, first, second), full, sems)
    normed, query_ref, key_ref, value_ref = (out.ref for out in (normed_out, query_out, key_out, value_out))
    gain, x_ref, beside_ref = gain_ref()[...], x_ref(), beside_ref()

    def main(rows):
        normal, _ = ln_stats(x_ref[rows, :].astype(F32))
        normed[rows, :] = (normal * gain).astype(BF16)

    rows_loop(ROWS, 128, main)
    normal, _ = ln_stats(beside_ref[...].astype(F32))
    normed[ROWS:, :] = (normal * gain).astype(BF16)
    normed_out.send()
    for copy in copies:
        copy.wait()
    cos_ref, sin_ref = cos_ref(), sin_ref()
    lane = low_lanes(ROWS + HALF_WIN, HEAD_DIM)
    for j in range(9):
        cols = slice(j * 256, (j + 1) * 256)
        proj = mm(normed[...], full[:, cols])
        for side in range(2):
            tile = proj[:, side * 128 : (side + 1) * 128]
            if j < 6:
                tile = tile * cos_ref[...] + turned(tile, lane) * sin_ref[...]
            place = slice((j % 3) * 256 + side * 128, (j % 3) * 256 + (side + 1) * 128)
            if j < 3:
                query_ref[:, place] = (tile[:ROWS] * 0.125).astype(BF16)
            else:
                out_ref = key_ref if j < 6 else value_ref
                edge = tile[ROWS:].astype(BF16)
                out_ref[HALF_WIN : HALF_WIN + ROWS, place] = tile[:ROWS].astype(BF16)
                out_ref[:HALF_WIN, place] = edge
                out_ref[HALF_WIN + ROWS :, place] = edge
        if j == 2:
            query_out.send()
        if j == 5:
            key_out.send()


def attend_kernel(where_ref, q_ref, k_ref, v_ref, att_out, prob_out):
    att_ref, prob_ref = att_out.ref, prob_out.ref
    q_ref, k_ref, v_ref = q_ref(), k_ref(), v_ref()
    half = where_ref[0]
    low_q, low_k = low_lanes(TILE, 128), low_lanes(2 * TILE, 128)
    row = lax.broadcasted_iota(jnp.int32, (2 * TILE, 2 * TILE), 0) % TILE
    col = lax.broadcasted_iota(jnp.int32, (2 * TILE, 2 * TILE), 1)
    band = (col >= row) & (col <= row + 2 * HALF_WIN)

    def tile_step(t, carry):
        begin = jnp.where((half == 0) & (t == 0), HALF_WIN, 0)
        end = jnp.where((half == 1) & (t == ROWS // TILE - 1), 2 * TILE - HALF_WIN, 2 * TILE)
        allowed = band & (col >= begin) & (col < end)
        rows = pl.ds(pl.multiple_of(t * TILE, TILE), TILE)
        span = pl.ds(pl.multiple_of(t * TILE, TILE), 2 * TILE)
        for pair in range(HEADS // 2):
            lanes = slice(pair * 128, (pair + 1) * 128)
            q = q_ref[rows, lanes]
            zero = jnp.zeros_like(q)
            stacked = jnp.concatenate([jnp.where(low_q, q, zero), jnp.where(low_q, zero, q)], 0)
            scores = jnp.where(allowed, mm_nt(stacked, k_ref[span, lanes]), masked_value)
            raised = jnp.exp(scores - jnp.max(scores, axis=-1, keepdims=True))
            probs = (raised * (1.0 / jnp.sum(raised, axis=-1, keepdims=True))).astype(BF16)
            prob_ref[t, pair] = probs
            v = v_ref[span, lanes]
            none = jnp.zeros_like(v)
            att_ref[rows, lanes] = mm(
                jnp.concatenate([probs[:TILE], probs[TILE:]], 1),
                jnp.concatenate([jnp.where(low_k, v, none), jnp.where(low_k, none, v)], 0),
            ).astype(BF16)
        return carry

    lax.fori_loop(0, ROWS // TILE, tile_step, 0)


def mlp_kernel(where_ref, att_ref, x_ref, gain_ref, cot_ref, att_own, in_own, out_own, first, second,
               hidden_out, up_out, send_out, keep_out, layer_out,
               w_att, w_in, w_out, normed, mixed, act_s, gate_s, dmix_s, sems):
    att_copies = place_weight(where_ref, (att_own, first, second), w_att, sems.at[0])
    in_copies = place_weight(where_ref, (in_own, first, second), w_in, sems.at[1], 240, 3)
    out_copies = place_weight(where_ref, (out_own, first, second), w_out, sems.at[2], 96)
    core = where_ref[1]
    hidden_ref, d_up, layer_ref = hidden_out.ref, up_out.ref, layer_out.ref
    att_ref, x_ref, gain = att_ref(), x_ref(), gain_ref()[...]
    for copy in att_copies:
        copy.wait()
    for j in range(3):
        cols = slice(j * 256, (j + 1) * 256)
        hidden_ref[:, cols] = x_ref[:, cols].astype(F32) + mm(att_ref[...], w_att[:, cols])
    hidden_out.send()

    def normalize(rows):
        normal, _ = ln_stats(hidden_ref[rows, :])
        normed[rows, :] = (normal * gain).astype(BF16)

    rows_loop(ROWS, 128, normalize)
    cot_ref = cot_ref()
    for copy in in_copies + out_copies:
        copy.wait()
    for j in range(3):
        cols = slice(j * 384, (j + 1) * 384)
        gates = slice(FF + j * 384, FF + (j + 1) * 384)
        act_s[...] = mm(normed[...], w_in[:, cols])
        gate_s[...] = mm(normed[...], w_in[:, gates])
        dmix_s[...] = mm_nt(cot_ref[...], w_out[cols, :])

        def gate(rows):
            act, gated_by, d_mixed = act_s[rows, :], gate_s[rows, :], dmix_s[rows, :]
            cumulative = 0.5 * (1.0 + lax.erf(act * 0.7071067811865476))
            density = jnp.exp(-0.5 * act * act) * 0.3989422804014327
            curved = act * cumulative
            mixed[rows, cols] = (curved * gated_by).astype(BF16)
            d_up[rows, cols] = (d_mixed * gated_by * (cumulative + act * density)).astype(BF16)
            d_up[rows, gates] = (d_mixed * curved).astype(BF16)

        rows_loop(ROWS, 128, gate)
    up_out.send()
    for out, which in ((send_out, 1 - core), (keep_out, core)):
        for j in range(3):
            cols = pl.ds(pl.multiple_of(which * 1152 + j * 384, 128), 384)
            grad = mm_tn(normed[...], d_up[:, cols]).astype(BF16)
            out.ref[:, :, j * 96 : (j + 1) * 96] = grad.reshape(2, 4, 96, 384)
        cols = pl.ds(pl.multiple_of(which * 384, 128), 384)
        grad = mm_tn(mixed[...], cot_ref[:, cols]).astype(BF16)
        out.ref[:, :, 288:] = grad.reshape(2, 4, 144, 384)
        out.send()
    for j in range(3):
        cols = slice(j * 256, (j + 1) * 256)
        layer_ref[:, cols] = (hidden_ref[:, cols] + mm(mixed[...], w_out[:, cols])).astype(BF16)


def mlp_back_kernel(where_ref, up_ref, hidden_ref, cot_ref, gain_ref, in_own, first, second,
                    dhid_out, w_in, dnorm_s, sems):
    copies = place_weight(where_ref, (in_own, first, second), w_in, sems, 240, 3)
    d_up = up_ref()
    for copy in copies:
        copy.wait()
    for j in range(3):
        cols = slice(j * 256, (j + 1) * 256)
        dnorm_s[:, cols] = mm_nt(d_up[...], w_in[cols, :])
    hidden_ref, cot_ref, gain = hidden_ref(), cot_ref(), gain_ref()[...]

    def back(rows):
        normal, scale = ln_stats(hidden_ref[rows, :])
        dhid_out.ref[rows, :] = cot_ref[rows, :].astype(F32) + ln_back(dnorm_s[rows, :], gain, normal, scale)

    rows_loop(ROWS, 128, back)


def attend_back_kernel(where_ref, dhid_ref, q_ref, k_ref, v_ref, prob_ref, cos_ref, sin_ref, att_ref, normed_ref,
                       own, first, second, dproj_out, edge_out, send_out, keep_out,
                       full, branch, datt, dkey, dvalue, grads_s, sems):
    copies = place_weight(where_ref, (own, first, second), full, sems)
    half, core = where_ref[0], where_ref[1]
    dproj_ref, edge_ref = dproj_out.ref, edge_out.ref
    dkey[...] = jnp.zeros_like(dkey)
    dvalue[...] = jnp.zeros_like(dvalue)
    for copy in copies:
        copy.wait()
    branch[...] = dhid_ref()[...].astype(BF16)
    for j in range(3):
        cols = slice(j * 256, (j + 1) * 256)
        datt[:, cols] = mm_nt(branch[...], full[cols, :]).astype(BF16)
    q_ref, k_ref, v_ref, prob_ref, cos_ref, sin_ref = (
        ref() for ref in (q_ref, k_ref, v_ref, prob_ref, cos_ref, sin_ref)
    )
    low_q, low_k = low_lanes(TILE, 128), low_lanes(2 * TILE, 128)
    turn_q = low_lanes(TILE, HEAD_DIM)

    def split(tile, low, axis=0):
        none = jnp.zeros_like(tile)
        return jnp.concatenate([jnp.where(low, tile, none), jnp.where(low, none, tile)], axis)

    def tile_step(t, carry):
        rows = pl.ds(pl.multiple_of(t * TILE, TILE), TILE)
        span = pl.ds(pl.multiple_of(t * TILE, TILE), 2 * TILE)
        cos, sin = cos_ref[rows, :], sin_ref[rows, :]
        for pair in range(HEADS // 2):
            lanes = slice(pair * 128, (pair + 1) * 128)
            grads = split(datt[rows, lanes], low_q)
            probs_b = prob_ref[t, pair]
            probs = probs_b.astype(F32)
            d_probs = mm_nt(grads, v_ref[span, lanes])
            delta = jnp.sum(probs * d_probs, axis=-1, keepdims=True)
            d_scores = (probs * (d_probs - delta)).astype(BF16)
            d_query = 0.125 * mm(
                jnp.concatenate([d_scores[:TILE], d_scores[TILE:]], 1), split(k_ref[span, lanes], low_k)
            )
            dproj_ref[rows, lanes] = (d_query * cos - turned(d_query, turn_q) * sin).astype(BF16)
            dkey[span, lanes] += mm_tn(d_scores, split(q_ref[rows, lanes], low_q))
            dvalue[span, lanes] += mm_tn(probs_b, grads)
        return carry

    lax.fori_loop(0, ROWS // TILE, tile_step, 0)
    turn_k = low_lanes(ROWS, HEAD_DIM)
    turn_e = low_lanes(HALF_WIN, HEAD_DIM)
    edge = pl.ds(pl.multiple_of((1 - half) * (ROWS + HALF_WIN), HALF_WIN), HALF_WIN)
    for pair in range(HEADS // 2):
        lanes = slice(pair * 128, (pair + 1) * 128)
        tile = dkey[HALF_WIN : HALF_WIN + ROWS, lanes]
        dproj_ref[:, 768 + pair * 128 : 768 + (pair + 1) * 128] = (
            tile * cos_ref[:ROWS] - turned(tile, turn_k) * sin_ref[:ROWS]
        ).astype(BF16)
        dproj_ref[:, 1536 + pair * 128 : 1536 + (pair + 1) * 128] = dvalue[
            HALF_WIN : HALF_WIN + ROWS, lanes
        ].astype(BF16)
        tile = dkey[edge, lanes]
        edge_ref[:, lanes] = (tile * cos_ref[ROWS:] - turned(tile, turn_e) * sin_ref[ROWS:]).astype(BF16)
        edge_ref[:, 768 + pair * 128 : 768 + (pair + 1) * 128] = dvalue[edge, lanes].astype(BF16)
    edge_out.send()
    dproj_out.send()
    normed_ref, att_ref = normed_ref(), att_ref()
    grads_s[:ROWS, :] = dproj_ref[...]
    grads_s[ROWS:, :768] = jnp.zeros((HALF_WIN, 768), BF16)
    grads_s[ROWS:, 768:] = edge_ref[...]
    for out, which in ((send_out, 1 - core), (keep_out, core)):
        for j in range(3):
            cols = pl.ds(pl.multiple_of(which * 1152 + j * 384, 128), 384)
            grad = mm_tn(normed_ref[...], grads_s[:, cols]).astype(BF16)
            out.ref[:, :, j * 96 : (j + 1) * 96] = grad.reshape(2, 4, 96, 384)
        cols = pl.ds(pl.multiple_of(which * 384, 128), 384)
        grad = mm_tn(att_ref[...], branch[:, cols]).astype(BF16)
        out.ref[:, :, 288:] = grad.reshape(2, 4, 96, 384)
        out.send()


def token_grad_kernel(where_ref, x_ref, gain_ref, dproj_ref, edge_ref, dhid_ref, own, first, second,
                      out, full, dnorm, sems):
    copies = place_weight(where_ref, (own, first, second), full, sems)
    grads, edge_ref = dproj_ref(), edge_ref()
    edge = pl.ds(pl.multiple_of((1 - where_ref[0]) * (ROWS - HALF_WIN), HALF_WIN), HALF_WIN)
    grads[edge, 768:] = (grads[edge, 768:].astype(F32) + edge_ref[...].astype(F32)).astype(BF16)
    for copy in copies:
        copy.wait()
    for j in range(3):
        cols = slice(j * 256, (j + 1) * 256)
        dnorm[:, cols] = mm_nt(grads[...], full[cols, :])

    gain, x_ref, dhid_ref = gain_ref()[...], x_ref(), dhid_ref()

    def back(rows):
        normal, scale = ln_stats(x_ref[rows, :].astype(F32))
        out.ref[rows, :] = (dhid_ref[rows, :] + ln_back(dnorm[rows, :], gain, normal, scale)).astype(BF16)

    rows_loop(ROWS, 128, back)


def finish_kernel(where_ref, mine, other, weight, gain, wide_out, narrow_out, gain_out):
    core = where_ref[1]
    wide_ref, narrow_ref = wide_out.ref, narrow_out.ref
    rows = narrow_ref.shape[0]
    for staged, which in ((mine, core), (other, 1 - core)):
        source = staged()
        for j in range(3):
            cols = pl.ds(pl.multiple_of(which * 1152 + j * 384, 128), 384)
            wide_ref[:, cols] = source[:, j * 96 : (j + 1) * 96].reshape(384, 384).astype(F32)
        cols = pl.ds(pl.multiple_of(which * 384, 128), 384)
        narrow_ref[:, cols] = source[:, 288:].reshape(rows, 384).astype(F32)
    wide_out.send()
    narrow_out.send()
    gain_rows(wide_ref, weight(), gain(), gain_out.ref)


def gain_rows(grad_ref, weight, gain, gain_ref):
    for n in range(3):
        rows = slice(n * 128, (n + 1) * 128)
        total = jnp.sum(grad_ref[rows, :] * weight[rows, :].astype(F32), axis=-1, keepdims=True)
        gain_ref[rows] = (jnp.broadcast_to(total, (128, 128)).T[:1] / gain[:, rows].astype(F32))[0]


class Staged:
    def __init__(self, source, ref, sem):
        self.ref, self.copy, self.there = ref, pltpu.make_async_copy(source, ref, sem), False
        self.copy.start()

    def __call__(self):
        if not self.there:
            self.copy.wait()
            self.there = True
        return self.ref


class Result:
    def __init__(self, ref, target, sem):
        self.ref, self.copy, self.sent = ref, pltpu.make_async_copy(ref, target, sem), False

    def send(self):
        if not self.sent:
            self.copy.start()
            self.sent = True


def run(kernel, ins, outs, scratch, flops):
    staged = [a for a, kind in ins if kind == "v"]
    spaces = {"s": pltpu.SMEM, "h": pl.ANY, "v": pl.ANY}
    moved = sum(a.size * a.dtype.itemsize for a, _ in ins) + sum(
        math.prod(shape) * jnp.dtype(dtype).itemsize for shape, dtype in outs
    )

    def body(*refs):
        given, refs = refs[: len(ins)], refs[len(ins) :]
        targets, refs = refs[: len(outs)], refs[len(outs) :]
        places, refs = refs[: len(staged)], refs[len(staged) :]
        ready, refs = refs[: len(outs)], refs[len(outs) :]
        in_sems, out_sems, *rest = refs
        taken, n = [], 0
        for ref, (_, kind) in zip(given, ins):
            if kind == "v":
                ref = Staged(ref, places[n], in_sems.at[n])
                n += 1
            taken.append(ref)
        results = [Result(r, t, out_sems.at[k]) for k, (r, t) in enumerate(zip(ready, targets))]
        kernel(*taken, *results, *rest)
        for ref in taken:
            if isinstance(ref, Staged):
                ref()
        for result in results:
            result.send()
        for result in results:
            result.copy.wait()

    dma = pltpu.SemaphoreType.DMA
    return pl.pallas_call(
        body,
        in_specs=[pl.BlockSpec(memory_space=spaces[kind]) for _, kind in ins],
        out_specs=[pl.BlockSpec(memory_space=pl.ANY) for _ in outs],
        out_shape=[jax.ShapeDtypeStruct(shape, dtype) for shape, dtype in outs],
        scratch_shapes=[pltpu.VMEM(a.shape, a.dtype) for a in staged]
        + [pltpu.VMEM(shape, dtype) for shape, dtype in outs]
        + [dma((len(staged),)), dma((len(outs),))]
        + scratch,
        compiler_params=pltpu.CompilerParams(vmem_limit_bytes=60 * 1024 * 1024),
        cost_estimate=pl.CostEstimate(flops=int(flops), bytes_accessed=int(moved), transcendentals=0),
    )(*[a for a, _ in ins])


def together(*arrays):
    return lax.optimization_barrier(arrays)


def block_of(own):
    rows, cols = own.shape
    index = lax.axis_index(CORE) * 2 + (lax.axis_index(XAXIS) & 1)
    return pick(own.reshape(4, rows // 4, cols), index, 0)


def beside_x(block, come):
    return ordered(block, come, lax.axis_index(XAXIS) & 1, 0)


def total_rows(send, keep, shape, first_axis, last_axis):
    core, half = lax.axis_index(CORE), lax.axis_index(FAR)
    near, place = lax.axis_index(NEAR) ^ half, lax.axis_index(first_axis)
    first_bit = jnp.where(core == 0, ((place + 1) >> 1) & 1, place >> 1)
    second_bit = place & 1
    send = yield send
    keep, come = keep.reshape(shape), core_swap(send).reshape(shape)
    for bit, first in ((first_bit, True), (second_bit, False)):
        send = yield add(pick(keep, 1 - bit, 1), pick(come, 1 - bit, 1))
        keep, come = add(pick(keep, bit, 1), pick(come, bit, 1)), ring_swap(send, first_axis, first)
    keep, come = (a.reshape((4,) + shape[4:]) for a in (keep, come))

    def two(which_half, which_near):
        index = [jnp.where(core == 0, which_half * 2 + i, i * 2 + which_near) for i in range(2)]
        return jnp.stack([add(pick(keep, i, 0), pick(come, i, 0)) for i in index])

    send = yield two(1 - half, 1 - near)
    keep, come = two(half, near), depth_swap(send, True)
    bit = jnp.where(core == 0, near, half)
    send = yield add(pick(keep, 1 - bit, 0), pick(come, 1 - bit, 0))
    keep, come = add(pick(keep, bit, 0), pick(come, bit, 0)), depth_swap(send, False)
    for first in (True, False):
        send = yield add(keep, come)
        keep, come = send, ring_swap(send, last_axis, first)
    send = yield add(keep, come)
    send = yield ordered(send, lax.ppermute(send, NEAR, SWAP), near, 0)
    send = yield ordered(send, ring_swap(send, first_axis, False), second_bit, 0)
    come = yield ring_swap(send, first_axis, True)
    send = yield ordered(send, come, first_bit, 0)
    yield send, core_swap(send)


def local(tokens, norm_gain_one, qkv_weight, attn_out_weight, norm_gain_two, in_weight, mlp_out_weight, cotangent):
    core, half = lax.axis_index(CORE), lax.axis_index(FAR)
    where = jnp.stack([half, core]).astype(jnp.int32)
    block = across_halves(block_of(qkv_weight))
    in_own = block_of(in_weight)
    rest_own = jnp.concatenate(
        [block_of(attn_out_weight), block_of(mlp_out_weight)] + [in_own[:, n * 768 : (n + 1) * 768] for n in range(3)], 0
    )
    edge = jnp.where(half == 0, tokens[ROWS - HALF_WIN :], tokens[:HALF_WIN])
    gains = jnp.pad(jnp.stack([norm_gain_one, norm_gain_two]), ((0, 14), (0, 384)))
    edge, rest_own = together(jnp.concatenate([edge, gains], 0), rest_own)
    beside = lax.ppermute(edge, FAR, SWAP)
    block, rest_own = together(block, rest_own)
    rest = across_halves(rest_own)
    both = beside_x(block, ring_swap(block, XAXIS, True))
    qkv = (qkv_weight, both, core_swap(both))
    fetched = beside[HALF_WIN:, :384]
    beside = beside[:HALF_WIN]
    gain_one = ordered(norm_gain_one, fetched[0], half, 0).reshape(1, 768).astype(F32)
    gain_two = ordered(norm_gain_two, fetched[1], half, 0).reshape(1, 768).astype(F32)
    index = jnp.arange(ROWS + HALF_WIN, dtype=jnp.int32)
    position = jnp.where(index < ROWS, half * ROWS + index, jnp.where(half == 0, index, index - HALF_WIN))
    lane = jnp.arange(128, dtype=jnp.int32)
    frequency = theta ** (-((lane % 32).astype(F32) * 2.0 / HEAD_DIM))
    angles = position.astype(F32)[:, None] * frequency[None, :]
    cosine = jnp.cos(angles)
    sine = jnp.where((lane % HEAD_DIM) < HEAD_DIM // 2, -1.0, 1.0) * jnp.sin(angles)

    h = lambda arrays: [(a, "h") for a in arrays]
    v = lambda *arrays: [(a, "v") for a in arrays]
    s = [(where, "s")]
    dma = pltpu.SemaphoreType.DMA
    wide, narrow, tall = pltpu.VMEM((768, 2304), BF16), pltpu.VMEM((768, 768), BF16), pltpu.VMEM((1152, 768), BF16)
    normed, query, key, value = run(
        qkv_kernel, s + v(tokens, beside, gain_one, cosine, sine) + h(qkv),
        [((ROWS + HALF_WIN, 768), BF16), ((ROWS, 768), BF16), ((640, 768), BF16), ((640, 768), BF16)],
        [wide, dma((5,))], 2 * 576 * 768 * 2304,
    )
    query, rest = together(query, rest)
    attended, probs = run(
        attend_kernel, s + v(query, key, value),
        [((ROWS, 768), BF16), ((4, 6, 256, 256), BF16)], [], 2 * 512 * 768 * 1024,
    )
    attended, come = together(attended, ring_swap(rest, XAXIS, True))
    both = beside_x(rest, come)
    rest = [both, core_swap(both)]
    hidden, d_up, send, keep, layer_output = run(
        mlp_kernel,
        s + v(attended, tokens, gain_two, cotangent) + h([attn_out_weight, in_weight, mlp_out_weight] + rest),
        [((ROWS, 768), F32), ((ROWS, 2 * FF), BF16), ((2, 4, 432, 384), BF16), ((2, 4, 432, 384), BF16),
         ((ROWS, 768), BF16)],
        [narrow, wide, tall, pltpu.VMEM((ROWS, 768), BF16), pltpu.VMEM((ROWS, FF), BF16),
         pltpu.VMEM((ROWS, 384), F32), pltpu.VMEM((ROWS, 384), F32), pltpu.VMEM((ROWS, 384), F32), dma((3, 13))],
        2 * 512 * 768 * 6600,
    )
    early = total_rows(send, keep, (2, 2, 2, 2, 216, 384), YAXIS, XAXIS)
    early_next = early.send(early.send(None))
    (d_hidden,) = run(
        mlp_back_kernel, s + v(d_up, hidden, cotangent, gain_two) + h([in_weight] + rest),
        [((ROWS, 768), F32)], [wide, pltpu.VMEM((ROWS, 768), F32), dma((13,))], 2 * 512 * 768 * 2304,
    )
    early_sent, d_hidden = together(early_next, d_hidden)
    early_next = early.send(early_sent)
    d_projected, edge_grad, send, keep = run(
        attend_back_kernel,
        s + v(d_hidden, query, key, value, probs, cosine, sine, attended, normed) + h([attn_out_weight] + rest),
        [((ROWS, 2304), BF16), ((HALF_WIN, 1536), BF16), ((2, 4, 384, 384), BF16), ((2, 4, 384, 384), BF16)],
        [narrow, pltpu.VMEM((ROWS, 768), BF16), pltpu.VMEM((ROWS, 768), BF16), pltpu.VMEM((640, 768), F32),
         pltpu.VMEM((640, 768), F32), pltpu.VMEM((ROWS + HALF_WIN, 2304), BF16), dma((5,))],
        2 * 512 * 768 * (768 + 2048 + 2304 + 768),
    )
    late = total_rows(send, keep, (2, 2, 2, 2, 192, 384), XAXIS, YAXIS)
    late_sent, early_sent = together(late.send(None), early_next)
    edge_grad = lax.ppermute(edge_grad, FAR, SWAP)
    early_next = early.send(early_sent)
    late_sent, edge_grad = together(late.send(late_sent), edge_grad)
    (token_grad,) = run(
        token_grad_kernel, s + v(tokens, gain_one, d_projected, edge_grad, d_hidden) + h(qkv),
        [((ROWS, 768), BF16)],
        [wide, pltpu.VMEM((ROWS, 768), F32), dma((5,))], 2 * 512 * 768 * 2304,
    )
    late_next, early_next, token_grad = together(late.send(late_sent), early_next, token_grad)
    for _ in range(6):
        late_next, early_next = together(late.send(late_next), early.send(early_next))
    early_next = early.send(early.send(early_next))
    late_next, early_next = together(late.send(late_next), early_next)
    early_next = early.send(early_next)

    def finish(pair, weight, gain, rows):
        return run(
            finish_kernel,
            s + v(*(a.reshape(4, -1, 384) for a in pair), weight, gain.reshape(1, 384)),
            [((384, 2304), F32), ((rows, 768), F32), ((384,), F32)], [], 0,
        )

    for _ in range(2):
        late_next = late.send(late_next)
    late_next, early_mine, early_other = together(late_next, *early_next)
    in_sum, mlp_out_sum, gain_two_sum = finish((early_mine, early_other), in_weight, norm_gain_two, 576)
    late_next = late.send(late_next)
    qkv_sum, attn_out_sum, gain_one_sum = finish(late_next, qkv_weight, norm_gain_one, 384)
    return (
        layer_output,
        token_grad,
        gain_one_sum,
        qkv_sum,
        attn_out_sum,
        gain_two_sum,
        in_sum,
        mlp_out_sum,
    )


def solution(mesh):
    fine = jax.sharding.Mesh(
        mesh.devices.reshape(4, 4, 2, 2, 2), (YAXIS, XAXIS, NEAR, CORE, FAR)
    )
    every = P((YAXIS, XAXIS, NEAR, CORE, FAR), None)
    return jax.shard_map(
        local,
        mesh=fine,
        in_specs=(every, P(FAR), P(FAR, None), P(FAR, None), P(FAR), P(FAR, None), P(FAR, None), every),
        out_specs=(every, every, P(FAR), P(FAR, None), P(FAR, None), P(FAR), P(FAR, None), P(FAR, None)),
        check_vma=False,
    )
```
